512 devices in a mesh: attn: 32 (over z, core), frow: 4 (over y), fcol: 4 (over x).
Axes of the slice: x: 4, y: 4, z: 16, core: 2. Of those that a mesh axis runs over, the one named last changes fastest.
Arguments:
- query_rows: bfloat16 [384, 8192], P(('attn', 'fcol'), 'frow'), may hold values from -10 to 10
- kv_cache: bfloat16 [2, 384, 1024, 512], P(None, ('attn', 'fcol'), None, 'frow'), may hold values from -16 to 16
- lengths: int32 [384], P(('attn', 'fcol')), may hold values from 1 to 1024, as said below
- residual: bfloat16 [384, 8192], P(('attn', 'fcol'), 'frow'), may hold values from -40 to 40
- norm_gain: float32 [8192], P('frow'), may hold values from 0.1 to 1.9
- w_gate_up: bfloat16 [2, 32768, 8192], P(None, ('attn', 'fcol'), 'frow'), may hold values from -0.0625 to 0.0625
- w_down: bfloat16 [32768, 8192], P(('attn', 'fcol'), 'frow'), may hold values from -0.03125 to 0.03125
Outputs:
- ffn_out: bfloat16 [384, 8192], P(('attn', 'fcol'), 'frow')
The draws below stay inside these ranges and needn't reach their ends.
Inputs may be any that keep to these rules, and one draw needn't show every extreme that they name: `lengths`: some row has all 1024 positions filled.
All inputs are finite; a program needn't handle non-finite values.
Results may differ from the reference program's by a relative error of at most 0.014.
Values may be sent and summed in bfloat16 or wider, within the bound.
A program may use at most 64 MiB of HBM per device.

```python
import math
import jax
import jax.numpy as jnp
from jax import lax

HD = 128
GROUP = 16
KVH = 4
FF = 32768
CACHE = 1024
D = 8192
ROWS = 384


def cache_lengths(key):
    length_key = jax.random.fold_in(key, 101)
    drawn_lengths = jax.random.randint(length_key, (ROWS,), 1, CACHE + 1)
    full_row = jax.random.randint(jax.random.fold_in(length_key, 1), (), 0, ROWS)
    return jnp.where(jnp.arange(ROWS) == full_row, CACHE, drawn_lengths).astype(jnp.int32)


def draw_lengths(key, part):
    return cache_lengths(key)


def draw_query_rows(key, part):
    own_key = jax.random.fold_in(key, 3)
    drawn_draw = jnp.clip(jax.random.normal(own_key, (ROWS, D)), -6.0, 6.0)
    return drawn_draw.astype(jnp.bfloat16)


def draw_kv_cache(key, part):
    own_key = jax.random.fold_in(key, 4)
    key_part, value_part = jax.random.split(own_key, 2)
    cache_shape = (ROWS, CACHE, KVH, HD)
    keys_drawn = jnp.clip(jax.random.normal(key_part, cache_shape), -6.0, 6.0)
    values_drawn = 3.0 * jnp.clip(jax.random.normal(value_part, cache_shape), -5.0, 5.0)
    stacked = jnp.stack([keys_drawn.reshape(ROWS, CACHE, KVH * HD), values_drawn.reshape(ROWS, CACHE, KVH * HD)])
    return stacked.astype(jnp.bfloat16)


def draw_residual(key, part):
    own_key = jax.random.fold_in(key, 5)
    row_key, col_key, drawn_key = jax.random.split(own_key, 3)
    row_scale = jnp.exp(jax.random.uniform(row_key, (ROWS, 1), minval=math.log(0.3), maxval=math.log(3.0)))
    col_ramp = 1.0 + 2.0 * jnp.arange(D, dtype=jnp.float32)[None, :] / D
    col_scale = col_ramp * jnp.exp(jax.random.uniform(col_key, (1, D), minval=math.log(0.3), maxval=0.0))
    drawn_draw = jnp.clip(jax.random.normal(drawn_key, (ROWS, D)), -4.0, 4.0)
    return (drawn_draw * row_scale * col_scale).astype(jnp.bfloat16)


def block_scale(rng, extent, pieces, low, high):
    def one(dim, parts):
        steps = jax.random.uniform(jax.random.fold_in(jax.random.fold_in(rng, 6), dim), (parts,), jnp.float32, low / len(pieces), high / len(pieces))
        return jnp.repeat(jnp.exp(steps), extent[dim] // parts).reshape((-1,) + (1,) * (len(extent) - dim - 1))

    factor_of = one(*pieces[0])
    for cut in pieces[1:]:
        factor_of = factor_of * one(*cut)
    return factor_of


def centred(key, dims, scale, limit, cuts=(), held_as=jnp.bfloat16):
    level = block_scale(key, dims, cuts, -0.22, 0.18) if cuts else 1.0
    array = jax.random.normal(key, dims, jnp.float32) * scale * level
    return jnp.minimum(jnp.maximum(array, -limit), limit).astype(held_as)


def setup_inputs(seed: int = 0) -> dict:
    keys = jax.random.split(jax.random.key(seed), 8)
    return {
        "query_rows": draw_query_rows(jax.random.fold_in(keys[7], 71), 0),
        "kv_cache": draw_kv_cache(jax.random.fold_in(keys[7], 71), 0),
        "lengths": draw_lengths(jax.random.fold_in(keys[7], 71), 0),
        "residual": draw_residual(jax.random.fold_in(keys[7], 71), 0),
        "norm_gain": jnp.clip(1.0 + 0.18 * jax.random.normal(keys[4], (D,), jnp.float32), 0.1, 1.9),
        "w_gate_up": centred(keys[5], (2, FF, D), D ** -0.5, 0.0625, ((1, 128), (2, 4))),
        "w_down": centred(keys[6], (FF, D), FF ** -0.5, 0.03125, ((0, 128), (1, 4))),
    }


def reference(query_rows, kv_cache, lengths, residual, norm_gain, w_gate_up, w_down):
    row_count = query_rows.shape[0]
    head_count = kv_cache.shape[3] // HD
    cache_span = kv_cache.shape[2]
    queries = query_rows.astype(jnp.float32).reshape(row_count, head_count, GROUP, HD)
    keys_here = kv_cache[0].astype(jnp.float32).reshape(row_count, cache_span, head_count, HD)
    values_here = kv_cache[1].astype(jnp.float32).reshape(row_count, cache_span, head_count, HD)
    scores = jnp.einsum('bgqd,bpgd->bgqp', queries, keys_here) / math.sqrt(HD)
    live_mask = (jnp.arange(cache_span, dtype=jnp.int32)[None, :] < lengths[:, None])[:, None, None, :]
    scores = jnp.where(live_mask, scores, -1e+30)
    row_top = lax.optimization_barrier(jnp.max(scores, axis=-1, keepdims=True))
    weights = jnp.where(live_mask, jnp.exp(scores - row_top), 0.0)
    denominator = lax.optimization_barrier(jnp.sum(weights, axis=-1))
    rounded = lax.optimization_barrier(weights.astype(jnp.bfloat16)).astype(jnp.float32)
    numerator = jnp.einsum('bgqp,bpgd->bgqd', rounded, values_here)
    attended = (numerator / denominator[..., None]).reshape(row_count, -1)
    mixed_rows = residual.astype(jnp.float32) + attended
    meansq = lax.optimization_barrier(jnp.mean(mixed_rows * mixed_rows, axis=-1, keepdims=True))
    normed = (mixed_rows * norm_gain * lax.rsqrt(meansq + 1e-05)).astype(jnp.bfloat16)
    gate_part = jnp.dot(normed, w_gate_up[0].T, preferred_element_type=jnp.float32)
    up_part = jnp.dot(normed, w_gate_up[1].T, preferred_element_type=jnp.float32)
    hidden = (jax.nn.silu(gate_part) * up_part).astype(jnp.bfloat16)
    return jnp.dot(hidden, w_down, preferred_element_type=jnp.float32).astype(jnp.bfloat16)
```

```python
import functools
import math

import jax
import jax.numpy as jnp
from jax import lax
from jax.experimental import pallas as pl
from jax.experimental.pallas import tpu as pltpu
from jax.sharding import PartitionSpec as P

HD = 128
GROUP = 16
MESH = pl.DeviceIdType.MESH
NT = (((1,), (1,)), ((), ()))

Z_OFFSETS = (0, 1, -1, 2, -2, 3, -3, 4, -4, 5, -5, 6, -6, 7, -7, 8)
Z_SLOT = {o % 16: i for i, o in enumerate(Z_OFFSETS)}
R_OFFSETS = (0, 1, -1, 2)
R_SLOT = {o % 4: i for i, o in enumerate(R_OFFSETS)}
NEAR_RUNS = ((0, 0, 1), (0, 1, 3), (0, 3, 5), (0, 5, 8))
FAR_RUNS = ((1, 0, 1), (1, 1, 3), (1, 3, 5), (1, 5, 8))


def body(len_ref, q_ref, res_ref, gain_ref, kv_hbm, wgu_hbm, wd_hbm, out_ref,
         kv, wgu, wd, lay, xb, xt, gu, yr, hb, po, dr, xr, s1, zi, zacc, zf,
         local_sem, send_sem, recv_sem):
    attn = lax.axis_index("attn")
    y = lax.axis_index("frow")
    x = lax.axis_index("fcol")
    z, core = attn // 2, attn % 2

    def at_z(offset):
        return {"attn": ((z + offset + 16) % 16) * 2 + core}

    def at_x(offset):
        return {"fcol": (x + offset + 4) % 4}

    def at_y(offset):
        return {"frow": (y + offset + 4) % 4}

    other_core = {"attn": z * 2 + 1 - core}

    loads = [
        pltpu.make_async_copy(kv_hbm, kv, local_sem.at[0]),
        pltpu.make_async_copy(wgu_hbm, wgu, local_sem.at[1]),
        pltpu.make_async_copy(wd_hbm, wd, local_sem.at[2]),
    ]
    for load in loads:
        load.start()

    barrier = pltpu.get_barrier_semaphore()
    peers = [at_z(o) for o in (4, -4, 3, -3, 2, -2, 1, -1)]
    peers += [at_x(o) for o in R_OFFSETS[1:]] + [at_y(o) for o in R_OFFSETS[1:]] + [other_core]
    for peer in peers:
        pl.semaphore_signal(barrier, inc=1, device_id=peer, device_id_type=MESH)

    started = []

    def send(src, dst, peer):
        index = len(started)
        copy = pltpu.make_async_remote_copy(
            src_ref=src, dst_ref=dst, send_sem=send_sem.at[index], recv_sem=recv_sem.at[index],
            device_id=peer, device_id_type=MESH,
        )
        copy.start()
        started.append(copy)
        return copy

    def spread(rows):
        for r in range(3):
            for h in range(GROUP):
                lay[pl.ds(r * GROUP + h, 1), :] = rows[r:r + 1, h * HD:(h + 1) * HD]
        return lay[...]

    queries = spread(q_ref[...].astype(jnp.float32)).astype(jnp.bfloat16)
    residual = spread(res_ref[...].astype(jnp.float32))
    gain = gain_ref[...]
    inverse = 1.0 / (gain * gain)
    rows_i = lax.broadcasted_iota(jnp.int32, (256, 256), 0)
    cols_i = lax.broadcasted_iota(jnp.int32, (256, 256), 1)
    swap = jnp.where(cols_i == (rows_i & 15) * 16 + (rows_i >> 4), 1.0, 0.0).astype(jnp.bfloat16)
    loads[0].wait()
    positions = lax.broadcasted_iota(jnp.int32, (GROUP, kv.shape[2]), 1)
    for r in range(3):
        scores = lax.dot_general(
            queries[r * GROUP:(r + 1) * GROUP], kv[0, r], NT, preferred_element_type=jnp.float32
        ) * (1.0 / math.sqrt(HD))
        live = positions < len_ref[r]
        scores = jnp.where(live, scores, -1e30)
        top = jnp.max(scores, axis=1, keepdims=True)
        expo = jnp.where(live, jnp.exp(scores - top), 0.0)
        total = jnp.sum(expo, axis=1, keepdims=True)
        summed = jnp.dot(expo.astype(jnp.bfloat16), kv[1, r], preferred_element_type=jnp.float32)
        mixed = residual[r * GROUP:(r + 1) * GROUP] + summed / total
        xb[0, 0, 0, 0, r * GROUP:(r + 1) * GROUP, :] = (mixed * gain).astype(jnp.bfloat16)

    pl.semaphore_wait(barrier, len(peers))

    def slot(offset):
        index = Z_SLOT[offset % 16]
        return xb.at[0, index // 8, 0, index % 8]

    z_copy = {}
    for o in (4, -4, 3, -3, 2, -2, 1, -1):
        z_copy[-o % 16] = send(slot(0), slot(-o), at_z(o))

    x_copy = {}

    def hand_on_x(run):
        chunk, first, end = run
        for k in range(first, end):
            offset = Z_OFFSETS[chunk * 8 + k]
            if offset not in (0, 4, -4):
                z_copy[offset % 16].wait_recv()
        n = end - first
        x_copy[run] = [
            send(xb.at[0, chunk, 0, pl.ds(first, n)], xb.at[0, chunk, R_SLOT[-o % 4], pl.ds(first, n)], at_x(o))
            for o in R_OFFSETS[1:]
        ]

    core_copy = {}

    def hand_on_core(run):
        chunk, first, end = run
        for copy in x_copy[run]:
            copy.wait_recv()
        here = (chunk, slice(None), pl.ds(first, end - first))
        core_copy[run] = send(xb.at[(0,) + here], xb.at[(1,) + here], other_core)

    hand_on_x(NEAR_RUNS[0])
    hand_on_x(NEAR_RUNS[1])
    hand_on_x(NEAR_RUNS[2])
    z_copy[-4 % 16].wait_recv()
    for j in (4, 3, 2, 1):
        z_copy[-(4 + j) % 16] = send(slot(-4), slot(-(4 + j)), at_z(j))
    z_copy[4].wait_recv()
    for j in (3, 2, 1):
        z_copy[4 + j] = send(slot(4), slot(4 + j), at_z(-j))
    hand_on_x(NEAR_RUNS[3])
    hand_on_x(FAR_RUNS[0])
    hand_on_core(NEAR_RUNS[0])
    hand_on_core(NEAR_RUNS[1])
    hand_on_x(FAR_RUNS[1])
    hand_on_core(NEAR_RUNS[2])
    hand_on_x(FAR_RUNS[2])
    hand_on_core(NEAR_RUNS[3])
    hand_on_x(FAR_RUNS[3])

    def widen(chunk, p):
        flat = xb[p, chunk].reshape(6, 256, HD)
        squares = []
        for g in range(6):
            turned = jnp.dot(swap, flat[g], preferred_element_type=jnp.float32)
            acc = jnp.zeros((16, HD), jnp.float32)
            for h in range(GROUP):
                part = turned[h * 16:(h + 1) * 16]
                acc += part * part * inverse[h:h + 1]
                xt[chunk, pl.ds((p * 6 + g) * 16, 16), h * HD:(h + 1) * HD] = part.astype(jnp.bfloat16)
            squares.append(jnp.sum(acc, axis=1, keepdims=True))
        return jnp.concatenate(squares, axis=0)

    lanes = lax.broadcasted_iota(jnp.int32, (96, HD), 1)

    def project(chunk, squares):
        for p in range(2):
            high = squares[p].astype(jnp.bfloat16).astype(jnp.float32)
            both = jnp.where(lanes < 64, high, squares[p] - high).astype(jnp.bfloat16)
            gu[chunk, 2 * p:2 * p + 2, :, 512:640] = both.reshape(2, 48, HD)
        rows = xt[chunk]
        for k in range(2):
            part = lax.dot_general(rows, wgu[k], NT, preferred_element_type=jnp.float32)
            gu[chunk, :, :, k * 256:(k + 1) * 256] = part.astype(jnp.bfloat16).reshape(4, 48, 256)
        return [
            send(gu.at[chunk, (y + o + 4) % 4], yr.at[chunk, R_SLOT[-o % 4] - 1], at_y(o))
            for o in R_OFFSETS[1:]
        ]

    def activate(chunk, copies):
        for copy in copies:
            copy.wait_recv()
        v = gu[chunk, y].astype(jnp.float32)
        for i in range(3):
            v += yr[chunk, i].astype(jnp.float32)
        meansq = (v[:, 512:513] + v[:, 576:577]) * (1.0 / 8192)
        scale = lax.rsqrt(meansq + 1e-05)
        gate = v[:, :256] * scale
        up = v[:, 256:512] * scale
        hb[chunk, y] = (gate / (1.0 + jnp.exp(-gate)) * up).astype(jnp.bfloat16)
        return [send(hb.at[chunk, y], hb.at[chunk, y], at_y(o)) for o in R_OFFSETS[1:]]

    def down(chunk, copies):
        for copy in copies:
            copy.wait_recv()
        for p in (1, 0):
            rows = hb[chunk, 2 * p:2 * p + 2].reshape(96, 256)
            wide = jnp.dot(rows, wd[...], preferred_element_type=jnp.float32).astype(jnp.bfloat16)
            for g in range(6):
                tall = jnp.concatenate(
                    [wide[g * 16:(g + 1) * 16, h * HD:(h + 1) * HD] for h in range(GROUP)], axis=0
                )
                turned = jnp.dot(swap, tall, preferred_element_type=jnp.float32).astype(jnp.bfloat16)
                po[p, chunk, pl.ds(g * 256, 256), :] = turned
            if p == 1:
                copy = send(po.at[1, chunk], dr.at[chunk], other_core)
        return copy

    def reduce_core(chunk, copy):
        copy.wait_recv()
        po[0, chunk] = (po[0, chunk].astype(jnp.float32) + dr[chunk].astype(jnp.float32)).astype(jnp.bfloat16)
        return [
            send(po.at[0, chunk, pl.ds(R_SLOT[o % 4] * 384, 384)], xr.at[chunk, R_SLOT[-o % 4] - 1], at_x(o))
            for o in R_OFFSETS[1:]
        ]

    def reduce_x(chunk, copies):
        for copy in copies:
            copy.wait_recv()
        v = po[0, chunk, 0:384].astype(jnp.float32)
        for i in range(3):
            v += xr[chunk, i].astype(jnp.float32)
        s1[chunk] = v.astype(jnp.bfloat16).reshape(8, 48, HD)

    loads[1].wait()
    squares_0 = [widen(0, 0)]
    for run in FAR_RUNS[:3]:
        hand_on_core(run)
    for run in NEAR_RUNS:
        core_copy[run].wait_recv()
    squares_0.append(widen(0, 1))
    hand_on_core(FAR_RUNS[3])
    y_0 = project(0, squares_0)
    squares_1 = [widen(1, 0)]
    for run in FAR_RUNS:
        core_copy[run].wait_recv()
    squares_1.append(widen(1, 1))
    y_1 = project(1, squares_1)
    h_0 = activate(0, y_0)
    h_1 = activate(1, y_1)
    loads[2].wait()
    c_0 = down(0, h_0)
    c_1 = down(1, h_1)
    x_0 = reduce_core(0, c_0)
    x_1 = reduce_core(1, c_1)

    def sums(offset):
        index = Z_SLOT[offset % 16]
        return s1.at[index // 8, index % 8]

    last = []
    reduce_x(0, x_0)
    for i, o in enumerate((3, -3, 2, -2, 1, -1)):
        last.append(send(sums(o), zf.at[i], at_z(o)))
    reduce_x(1, x_1)
    ahead = [send(sums(4 + j), zi.at[j - 1], at_z(j)) for j in (4, 3, 2, 1)]
    behind = [send(sums(-4 - j), zi.at[3 + j], at_z(-j)) for j in (3, 2, 1)]
    for copies, offset, first, count, i in ((ahead, 4, 0, 4, 6), (behind, -4, 4, 3, 7)):
        for copy in copies:
            copy.wait_recv()
        v = sums(offset)[...].astype(jnp.float32)
        for j in range(count):
            v += zi[first + j].astype(jnp.float32)
        zacc[i - 6] = v.astype(jnp.bfloat16)
        last.append(send(zacc.at[i - 6], zf.at[i], at_z(offset)))
    v = sums(0)[...].astype(jnp.float32)
    for i, copy in enumerate(last):
        copy.wait_recv()
        v += zf[i].astype(jnp.float32)
    lay[...] = v
    for r in range(3):
        for h in range(GROUP):
            out_ref[r:r + 1, h * HD:(h + 1) * HD] = lay[pl.ds(r * GROUP + h, 1), :].astype(jnp.bfloat16)
    for copy in started:
        copy.wait_send()


def on_device(query_rows, kv_cache, lengths, residual, norm_gain, w_gate_up, w_down):
    bf16 = jnp.bfloat16
    vmem = pl.BlockSpec(memory_space=pltpu.VMEM)
    hbm = pl.BlockSpec(memory_space=pl.ANY)
    return pl.pallas_call(
        body,
        out_shape=jax.ShapeDtypeStruct(query_rows.shape, bf16),
        in_specs=[pl.BlockSpec(memory_space=pltpu.SMEM), vmem, vmem, vmem, hbm, hbm, hbm],
        out_specs=vmem,
        scratch_shapes=[
            pltpu.VMEM(kv_cache.shape, bf16),
            pltpu.VMEM(w_gate_up.shape, bf16),
            pltpu.VMEM(w_down.shape, bf16),
            pltpu.VMEM((48, HD), jnp.float32),
            pltpu.VMEM((2, 2, 4, 8, 48, HD), bf16),
            pltpu.VMEM((2, 192, 2048), bf16),
            pltpu.VMEM((2, 4, 48, 640), bf16),
            pltpu.VMEM((2, 3, 48, 640), bf16),
            pltpu.VMEM((2, 4, 48, 256), bf16),
            pltpu.VMEM((2, 2, 1536, HD), bf16),
            pltpu.VMEM((2, 1536, HD), bf16),
            pltpu.VMEM((2, 3, 384, HD), bf16),
            pltpu.VMEM((2, 8, 48, HD), bf16),
            pltpu.VMEM((7, 48, HD), bf16),
            pltpu.VMEM((2, 48, HD), bf16),
            pltpu.VMEM((8, 48, HD), bf16),
            pltpu.SemaphoreType.DMA((3,)),
            pltpu.SemaphoreType.DMA((96,)),
            pltpu.SemaphoreType.DMA((96,)),
        ],
        compiler_params=pltpu.CompilerParams(
            collective_id=0, has_side_effects=True, vmem_limit_bytes=40 * 1024 * 1024
        ),
        name="decode",
    )(lengths, query_rows, residual, norm_gain.reshape(GROUP, HD), kv_cache.reshape(2, 3, -1, HD), w_gate_up, w_down)


def solution(mesh):
    return jax.shard_map(
        on_device,
        mesh=mesh,
        in_specs=(
            P(("attn", "fcol"), "frow"),
            P(None, ("attn", "fcol"), None, "frow"),
            P(("attn", "fcol")),
            P(("attn", "fcol"), "frow"),
            P("frow"),
            P(None, ("attn", "fcol"), "frow"),
            P(("attn", "fcol"), "frow"),
        ),
        out_specs=P(("attn", "fcol"), "frow"),
        check_vma=False,
    )
```

```python
import functools
import math

import jax
import jax.numpy as jnp
from jax import lax
from jax.experimental import pallas as pl
from jax.experimental.pallas import tpu as pltpu
from jax.sharding import PartitionSpec as P

HD = 128
GROUP = 16
MESH = pl.DeviceIdType.MESH
SENDS, LANDS = 16, 37
NT = (((1,), (1,)), ((), ()))

Z_OFFSETS = (0, 1, -1, 2, -2, 3, -3, 4, -4, 5, -5, 6, -6, 7, -7, 8)
Z_SLOT = {o % 16: i for i, o in enumerate(Z_OFFSETS)}
R_OFFSETS = (0, 1, -1, 2)
R_SLOT = {o % 4: i for i, o in enumerate(R_OFFSETS)}
NEAR_RUNS = ((0, 0, 1), (0, 1, 3), (0, 3, 5), (0, 5, 8))
FAR_RUNS = ((1, 0, 1), (1, 1, 3), (1, 3, 5), (1, 5, 8))


def body(len_hbm, q_hbm, res_hbm, gain_hbm, kv_hbm, wgu_hbm, wd_hbm, out_ref,
         len_ref, q_ref, res_ref, gain_ref, kv, wgu, wd, lay, inverse, xb, xt, gu, yr, hb, po, dr, xr, s1, zi, zacc, zf, room,
         local_sem, send_sem, recv_sem):
    attn = lax.axis_index("attn")
    y = lax.axis_index("frow")
    x = lax.axis_index("fcol")
    z, core = attn // 2, attn % 2

    def at_z(offset):
        return {"attn": ((z + offset + 16) % 16) * 2 + core}

    def at_x(offset):
        return {"fcol": (x + offset + 4) % 4}

    def at_y(offset):
        return {"frow": (y + offset + 4) % 4}

    other_core = {"attn": z * 2 + 1 - core}

    barrier = pltpu.get_barrier_semaphore()
    peers = [at_z(o) for o in (4, -4, 3, -3, 2, -2, 1, -1)]
    peers += [at_x(o) for o in R_OFFSETS[1:]] + [at_y(o) for o in R_OFFSETS[1:]] + [other_core]
    for peer in peers:
        pl.semaphore_signal(barrier, inc=1, device_id=peer, device_id_type=MESH)

    operands = (
        (q_hbm, q_ref), (len_hbm, len_ref), (res_hbm, res_ref), (gain_hbm, gain_ref),
        (kv_hbm.at[0], kv.at[0]), (kv_hbm.at[1], kv.at[1]), (wgu_hbm, wgu), (wd_hbm, wd),
    )
    loads = [pltpu.make_async_copy(src, dst, local_sem.at[i]) for i, (src, dst) in enumerate(operands)]
    for load in loads:
        load.start()

    taken = [0, 0]
    sent = []

    def take(kind):
        taken[kind] += 1
        return (send_sem, recv_sem)[kind].at[taken[kind] - 1]

    def outgoing(rows):
        sent.append((take(0), rows))
        return sent[-1][0]

    def remote(src, dst, peer, leaves, lands):
        return pltpu.make_async_remote_copy(
            src_ref=src, dst_ref=dst, send_sem=leaves, recv_sem=lands, device_id=peer, device_id_type=MESH
        )

    def send(src, dst, peer, leaves, lands):
        remote(src, dst, peer, leaves, lands).start()

    def landed(ref, sem):
        pltpu.make_async_copy(ref, ref, sem).wait()

    def spread(rows):
        for r in range(3):
            for h in range(GROUP):
                lay[pl.ds(r * GROUP + h, 1), :] = rows[r:r + 1, h * HD:(h + 1) * HD]
        return lay[...]

    for load in loads[:4]:
        load.wait()
    queries = spread(q_ref[...].astype(jnp.float32)).astype(jnp.bfloat16)
    residual = spread(res_ref[...].astype(jnp.float32))
    gain = gain_ref[...]
    square = 1.0 / (gain * gain)
    for h in range(GROUP):
        inverse[:, h * HD:(h + 1) * HD] = square[h:h + 1]
    loads[4].wait()
    loads[5].wait()
    positions = lax.broadcasted_iota(jnp.int32, (GROUP, kv.shape[2]), 1)
    for r in range(3):
        scores = lax.dot_general(
            queries[r * GROUP:(r + 1) * GROUP], kv[0, r], NT, preferred_element_type=jnp.float32
        ) * (1.0 / math.sqrt(HD))
        live = positions < len_ref[r]
        scores = jnp.where(live, scores, -1e30)
        top = jnp.max(scores, axis=1, keepdims=True)
        expo = jnp.where(live, jnp.exp(scores - top), 0.0)
        total = jnp.sum(expo, axis=1, keepdims=True)
        summed = jnp.dot(expo.astype(jnp.bfloat16), kv[1, r], preferred_element_type=jnp.float32)
        mixed = residual[r * GROUP:(r + 1) * GROUP] + summed / total
        xb[0, 0, 0, 0, r * GROUP:(r + 1) * GROUP, :] = (mixed * gain).astype(jnp.bfloat16)

    pl.semaphore_wait(barrier, len(peers))

    def slot(offset):
        index = Z_SLOT[offset % 16]
        return xb.at[0, index // 8, 0, index % 8]

    z_sem = {}
    for group in ((1, -1), (2, -2), (3, -3), (4,), (-4,), (5, -5), (6, -6), (7, -7, 8)):
        lands = take(1)
        for o in group:
            z_sem[o % 16] = lands
    leaves = outgoing(15 * 48)
    for o in (4, -4, 3, -3, 2, -2, 1, -1):
        send(slot(0), slot(-o), at_z(o), leaves, z_sem[-o % 16])

    x_sem = {run: take(1) for run in NEAR_RUNS + FAR_RUNS}
    core_sem = {run: take(1) for run in NEAR_RUNS + FAR_RUNS}
    x_leaves = [outgoing(8 * 48 * 3), outgoing(8 * 48 * 3)]
    core_leaves = [outgoing(8 * 48 * 4), outgoing(8 * 48 * 4)]

    def along_z(run, count=None):
        chunk, first, end = run
        return xb.at[0, chunk, 0, pl.ds(first, (end - first) if count is None else count)]

    def hand_on_x(run):
        chunk, first, end = run
        if run == NEAR_RUNS[3]:
            landed(along_z(run, 2), z_sem[3])
        elif run not in (NEAR_RUNS[0], FAR_RUNS[0]):
            landed(along_z(run), z_sem[Z_OFFSETS[chunk * 8 + first] % 16])
        here = pl.ds(first, end - first)
        for o in (2, 1, -1):
            send(xb.at[0, chunk, 0, here], xb.at[0, chunk, R_SLOT[-o % 4], here], at_x(o), x_leaves[chunk], x_sem[run])

    def hand_on_core(run):
        chunk, first, end = run
        here = pl.ds(first, end - first)
        landed(xb.at[0, chunk, 1:4, here], x_sem[run])
        send(xb.at[0, chunk, :, here], xb.at[1, chunk, :, here], other_core, core_leaves[chunk], core_sem[run])

    def from_core(run):
        chunk, first, end = run
        landed(xb.at[1, chunk, :, pl.ds(first, end - first)], core_sem[run])

    hand_on_x(NEAR_RUNS[0])
    hand_on_x(NEAR_RUNS[1])
    hand_on_x(NEAR_RUNS[2])
    landed(slot(-4), z_sem[-4 % 16])
    for j in (4, 3, 2, 1):
        send(slot(-4), slot(-(4 + j)), at_z(j), leaves, z_sem[-(4 + j) % 16])
    landed(slot(4), z_sem[4])
    for j in (3, 2, 1):
        send(slot(4), slot(4 + j), at_z(-j), leaves, z_sem[4 + j])
    hand_on_x(NEAR_RUNS[3])
    hand_on_x(FAR_RUNS[0])
    hand_on_core(NEAR_RUNS[0])
    hand_on_core(NEAR_RUNS[1])
    hand_on_x(FAR_RUNS[1])
    hand_on_core(NEAR_RUNS[2])
    hand_on_x(FAR_RUNS[2])
    hand_on_core(NEAR_RUNS[3])
    hand_on_x(FAR_RUNS[3])

    def widen(chunk, p):
        rows = xb[p, chunk].reshape(96, GROUP, HD).reshape(96, GROUP * HD)
        xt[chunk, pl.ds(p * 96, 96), :] = rows
        wide = rows.astype(jnp.float32)
        return jnp.sum(wide * wide * inverse[...], axis=1, keepdims=True)

    lanes = lax.broadcasted_iota(jnp.int32, (96, HD), 1)
    y_sem = [(outgoing(720), take(1)) for _ in range(2)]
    h_sem = [(outgoing(288), take(1)) for _ in range(2)]

    def project(chunk, p, squares):
        high = squares.astype(jnp.bfloat16).astype(jnp.float32)
        both = jnp.where(lanes < 64, high, squares - high).astype(jnp.bfloat16)
        gu[chunk, 2 * p:2 * p + 2, :, 512:640] = both.reshape(2, 48, HD)
        rows = xt[chunk, p * 96:(p + 1) * 96]
        for k in range(2):
            part = lax.dot_general(rows, wgu[k], NT, preferred_element_type=jnp.float32)
            gu[chunk, 2 * p:2 * p + 2, :, k * 256:(k + 1) * 256] = part.astype(jnp.bfloat16).reshape(2, 48, 256)
        for o in (2, 1, -1):
            target = (y + o + 4) % 4
            copy = remote(gu.at[chunk, target], yr.at[chunk, R_SLOT[-o % 4] - 1], at_y(o), *y_sem[chunk])
            pl.when(target // 2 == p)(copy.start)

    def activate(chunk):
        landed(yr.at[chunk], y_sem[chunk][1])
        v = gu[chunk, y].astype(jnp.float32)
        for i in range(3):
            v += yr[chunk, i].astype(jnp.float32)
        meansq = (v[:, 512:513] + v[:, 576:577]) * (1.0 / 8192)
        scale = lax.rsqrt(meansq + 1e-05)
        gate = v[:, :256] * scale
        up = v[:, 256:512] * scale
        hb[chunk, y] = (gate / (1.0 + jnp.exp(-gate)) * up).astype(jnp.bfloat16)
        for o in (2, 1, -1):
            send(hb.at[chunk, y], hb.at[chunk, y], at_y(o), *h_sem[chunk])

    halves = ((slice(None),), (1, 0))
    c_sem = [[(outgoing(1536 // len(h)), take(1)) for _ in h] for h in halves]
    r_sem = [[(outgoing(1152 // len(h)), take(1)) for _ in h] for h in halves]

    def down(chunk):
        landed(hb.at[chunk, 0:3], h_sem[chunk][1])
        for p in (1, 0):
            rows = hb[chunk, 2 * p:2 * p + 2].reshape(96, 256)
            wide = jnp.dot(rows, wd[...], preferred_element_type=jnp.float32).astype(jnp.bfloat16)
            po[p, chunk] = wide.reshape(96, GROUP, HD).reshape(4, 2, 192, HD)
            if p == 1:
                for half, sems in zip(halves[chunk], c_sem[chunk]):
                    send(po.at[1, chunk, :, half], dr.at[chunk, :, half], other_core, *sems)

    def reduce_core(chunk):
        for half, sems, onward in zip(halves[chunk], c_sem[chunk], r_sem[chunk]):
            landed(dr.at[chunk, :, half], sems[1])
            v = po[0, chunk, :, half].astype(jnp.float32) + dr[chunk, :, half].astype(jnp.float32)
            po[0, chunk, :, half] = v.astype(jnp.bfloat16)
            for o in (2, 1, -1):
                send(po.at[0, chunk, R_SLOT[o % 4], half], xr.at[chunk, R_SLOT[-o % 4] - 1, half], at_x(o), *onward)

    def reduce_x(chunk, i):
        half = halves[chunk][i]
        landed(xr.at[chunk, :, half], r_sem[chunk][i][1])
        v = po[0, chunk, 0, half].astype(jnp.float32)
        for k in range(3):
            v += xr[chunk, k, half].astype(jnp.float32)
        s1[chunk, half] = v.astype(jnp.bfloat16).reshape(s1.at[chunk, half].shape)

    def sums(offset):
        index = Z_SLOT[offset % 16]
        return s1.at[index // 8, index // 4 % 2, index % 4]

    last_sem = (outgoing(15 * 48), take(1))
    far_sem = [(last_sem[0], take(1)) for _ in range(2)]

    loads[6].wait()
    squares = widen(0, 0)
    project(0, 0, squares)
    for run in NEAR_RUNS:
        from_core(run)
    squares = widen(0, 1)
    project(0, 1, squares)
    for run in FAR_RUNS:
        hand_on_core(run)
    activate(0)
    squares = widen(1, 0)
    project(1, 0, squares)
    for run in FAR_RUNS:
        from_core(run)
    squares = widen(1, 1)
    project(1, 1, squares)
    loads[7].wait()
    down(0)
    activate(1)
    reduce_core(0)
    down(1)
    reduce_core(1)
    reduce_x(0, 0)
    for i, o in enumerate((3, -3, 2, -2, 1, -1)):
        send(sums(o), zf.at[i], at_z(o), *last_sem)
    reduce_x(1, 0)
    for o in (8, 7, -7, -6):
        j = abs(o) - 4
        send(sums(o), zi.at[j - 1 if o > 0 else 3 + j], at_z(j if o > 0 else -j), *far_sem[0 if o > 0 else 1])
    reduce_x(1, 1)
    for o in (6, 5, -5):
        j = abs(o) - 4
        send(sums(o), zi.at[j - 1 if o > 0 else 3 + j], at_z(j if o > 0 else -j), *far_sem[0 if o > 0 else 1])
    for i, (offset, first, count) in enumerate(((4, 0, 4), (-4, 4, 3))):
        landed(zi.at[pl.ds(first, count)], far_sem[i][1])
        v = sums(offset)[...].astype(jnp.float32)
        for j in range(count):
            v += zi[first + j].astype(jnp.float32)
        zacc[i] = v.astype(jnp.bfloat16)
        send(zacc.at[i], zf.at[6 + i], at_z(offset), *last_sem)
    v = sums(0)[...].astype(jnp.float32)
    landed(zf, last_sem[1])
    for i in range(8):
        v += zf[i].astype(jnp.float32)
    lay[...] = v
    for r in range(3):
        for h in range(GROUP):
            out_ref[r:r + 1, h * HD:(h + 1) * HD] = lay[pl.ds(r * GROUP + h, 1), :].astype(jnp.bfloat16)
    for leaves, rows in sent:
        landed(room.at[pl.ds(0, rows)], leaves)
    assert taken == [SENDS, LANDS], taken


def on_device(query_rows, kv_cache, lengths, residual, norm_gain, w_gate_up, w_down):
    bf16 = jnp.bfloat16
    vmem = pl.BlockSpec(memory_space=pltpu.VMEM)
    hbm = pl.BlockSpec(memory_space=pl.ANY)
    return pl.pallas_call(
        body,
        out_shape=jax.ShapeDtypeStruct(query_rows.shape, bf16),
        in_specs=[hbm] * 7,
        out_specs=vmem,
        scratch_shapes=[
            pltpu.SMEM(lengths.shape, jnp.int32),
            pltpu.VMEM(query_rows.shape, bf16),
            pltpu.VMEM(residual.shape, bf16),
            pltpu.VMEM((GROUP, HD), jnp.float32),
            pltpu.VMEM(kv_cache.shape, bf16),
            pltpu.VMEM(w_gate_up.shape, bf16),
            pltpu.VMEM(w_down.shape, bf16),
            pltpu.VMEM((48, HD), jnp.float32),
            pltpu.VMEM((1, GROUP * HD), jnp.float32),
            pltpu.VMEM((2, 2, 4, 8, 48, HD), bf16),
            pltpu.VMEM((2, 192, 2048), bf16),
            pltpu.VMEM((2, 4, 48, 640), bf16),
            pltpu.VMEM((2, 3, 48, 640), bf16),
            pltpu.VMEM((2, 4, 48, 256), bf16),
            pltpu.VMEM((2, 2, 4, 2, 192, HD), bf16),
            pltpu.VMEM((2, 4, 2, 192, HD), bf16),
            pltpu.VMEM((2, 3, 2, 192, HD), bf16),
            pltpu.VMEM((2, 2, 4, 48, HD), bf16),
            pltpu.VMEM((7, 48, HD), bf16),
            pltpu.VMEM((2, 48, HD), bf16),
            pltpu.VMEM((8, 48, HD), bf16),
            pltpu.VMEM((1536, HD), bf16),
            pltpu.SemaphoreType.DMA((8,)),
            pltpu.SemaphoreType.DMA((SENDS,)),
            pltpu.SemaphoreType.DMA((LANDS,)),
        ],
        compiler_params=pltpu.CompilerParams(
            collective_id=0, has_side_effects=True, vmem_limit_bytes=60 * 1024 * 1024
        ),
        name="decode",
    )(lengths, query_rows, residual, norm_gain.reshape(GROUP, HD), kv_cache.reshape(2, 3, -1, HD), w_gate_up, w_down)


def solution(mesh):
    return jax.shard_map(
        on_device,
        mesh=mesh,
        in_specs=(
            P(("attn", "fcol"), "frow"),
            P(None, ("attn", "fcol"), None, "frow"),
            P(("attn", "fcol")),
            P(("attn", "fcol"), "frow"),
            P("frow"),
            P(None, ("attn", "fcol"), "frow"),
            P(("attn", "fcol"), "frow"),
        ),
        out_specs=P(("attn", "fcol"), "frow"),
        check_vma=False,
    )
```

```python
import functools
import math

import jax
import jax.numpy as jnp
from jax import lax
from jax.experimental import pallas as pl
from jax.experimental.pallas import tpu as pltpu
from jax.sharding import PartitionSpec as P

HD = 128
GROUP = 16
MESH = pl.DeviceIdType.MESH
SENDS, LANDS = 16, 40
NT = (((1,), (1,)), ((), ()))

Z_OFFSETS = (0, 1, -1, 2, -2, 3, -3, 4, -4, 5, -5, 6, -6, 7, -7, 8)
Z_SLOT = {o % 16: i for i, o in enumerate(Z_OFFSETS)}
R_OFFSETS = (0, 1, -1, 2)
R_SLOT = {o % 4: i for i, o in enumerate(R_OFFSETS)}
NEAR_RUNS = ((0, 0, 1), (0, 1, 3), (0, 3, 5), (0, 5, 8))
FAR_RUNS = ((1, 0, 1), (1, 1, 3), (1, 3, 5), (1, 5, 7), (1, 7, 8))


def body(len_hbm, q_hbm, res_hbm, gain_hbm, kv_hbm, wgu_hbm, wd_hbm, out_ref,
         len_ref, q_ref, res_ref, gain_ref, kv, wgu, wt, wd, lay, inverse, xb, xt, gu, yr, hb, po, dr, xr, s1, zi, zacc, zf, room,
         local_sem, send_sem, recv_sem):
    attn = lax.axis_index("attn")
    y = lax.axis_index("frow")
    x = lax.axis_index("fcol")
    z, core = attn // 2, attn % 2

    def at_z(offset):
        return {"attn": ((z + offset + 16) % 16) * 2 + core}

    def at_x(offset):
        return {"fcol": (x + offset + 4) % 4}

    def at_y(offset):
        return {"frow": (y + offset + 4) % 4}

    other_core = {"attn": z * 2 + 1 - core}

    barrier = pltpu.get_barrier_semaphore()
    peers = [at_z(o) for o in (4, -4, 3, -3, 2, -2, 1, -1)]
    peers += [at_x(o) for o in R_OFFSETS[1:]] + [at_y(o) for o in R_OFFSETS[1:]] + [other_core]
    for peer in peers:
        pl.semaphore_signal(barrier, inc=1, device_id=peer, device_id_type=MESH)

    operands = (
        (q_hbm, q_ref), (len_hbm, len_ref), (res_hbm, res_ref), (gain_hbm, gain_ref),
        (kv_hbm.at[0], kv.at[0]), (kv_hbm.at[1], kv.at[1]), (wgu_hbm, wgu), (wd_hbm, wd),
    )
    loads = [pltpu.make_async_copy(src, dst, local_sem.at[i]) for i, (src, dst) in enumerate(operands)]
    for load in loads:
        load.start()

    taken = [0, 0]
    sent = []

    def take(kind):
        taken[kind] += 1
        return (send_sem, recv_sem)[kind].at[taken[kind] - 1]

    def outgoing(rows):
        sent.append((take(0), rows))
        return sent[-1][0]

    def remote(src, dst, peer, leaves, lands):
        return pltpu.make_async_remote_copy(
            src_ref=src, dst_ref=dst, send_sem=leaves, recv_sem=lands, device_id=peer, device_id_type=MESH
        )

    def send(src, dst, peer, leaves, lands):
        remote(src, dst, peer, leaves, lands).start()

    def landed(ref, sem):
        pltpu.make_async_copy(ref, ref, sem).wait()

    def spread(rows):
        for r in range(3):
            for h in range(GROUP):
                lay[pl.ds(r * GROUP + h, 1), :] = rows[r:r + 1, h * HD:(h + 1) * HD]
        return lay[...]

    for load in loads[:4]:
        load.wait()
    queries = spread(q_ref[...].astype(jnp.float32)).astype(jnp.bfloat16)
    residual = spread(res_ref[...].astype(jnp.float32))
    gain = gain_ref[...]
    square = 1.0 / (gain * gain)
    for h in range(GROUP):
        inverse[:, h * HD:(h + 1) * HD] = square[h:h + 1]
    loads[4].wait()
    loads[5].wait()
    positions = lax.broadcasted_iota(jnp.int32, (GROUP, kv.shape[2]), 1)
    for r in range(3):
        scores = lax.dot_general(
            queries[r * GROUP:(r + 1) * GROUP], kv[0, r], NT, preferred_element_type=jnp.float32
        ) * (1.0 / math.sqrt(HD))
        live = positions < len_ref[r]
        scores = jnp.where(live, scores, -1e30)
        top = jnp.max(scores, axis=1, keepdims=True)
        expo = jnp.where(live, jnp.exp(scores - top), 0.0)
        total = jnp.sum(expo, axis=1, keepdims=True)
        summed = jnp.dot(expo.astype(jnp.bfloat16), kv[1, r], preferred_element_type=jnp.float32)
        mixed = residual[r * GROUP:(r + 1) * GROUP] + summed / total
        xb[0, 0, 0, 0, r * GROUP:(r + 1) * GROUP, :] = (mixed * gain).astype(jnp.bfloat16)

    pl.semaphore_wait(barrier, len(peers))

    def slot(offset):
        index = Z_SLOT[offset % 16]
        return xb.at[0, index // 8, 0, index % 8]

    z_sem = {}
    for group in ((1, -1), (2, -2), (3, -3), (4,), (-4,), (5, -5), (6, -6), (7, -7), (8,)):
        lands = take(1)
        for o in group:
            z_sem[o % 16] = lands
    leaves = outgoing(15 * 48)
    for o in (4, -4, 3, -3, 2, -2, 1, -1):
        send(slot(0), slot(-o), at_z(o), leaves, z_sem[-o % 16])

    x_sem = {run: take(1) for run in NEAR_RUNS + FAR_RUNS}
    core_sem = {run: take(1) for run in NEAR_RUNS + FAR_RUNS}
    x_leaves = [outgoing(8 * 48 * 3), outgoing(8 * 48 * 3)]
    core_leaves = [outgoing(8 * 48 * 4), outgoing(8 * 48 * 4)]

    def along_z(run, count=None):
        chunk, first, end = run
        return xb.at[0, chunk, 0, pl.ds(first, (end - first) if count is None else count)]

    def hand_on_x(run):
        chunk, first, end = run
        if run == NEAR_RUNS[3]:
            landed(along_z(run, 2), z_sem[3])
        elif run not in (NEAR_RUNS[0], FAR_RUNS[0]):
            landed(along_z(run), z_sem[Z_OFFSETS[chunk * 8 + first] % 16])
        here = pl.ds(first, end - first)
        for o in (2, 1, -1):
            send(xb.at[0, chunk, 0, here], xb.at[0, chunk, R_SLOT[-o % 4], here], at_x(o), x_leaves[chunk], x_sem[run])

    def hand_on_core(run):
        chunk, first, end = run
        here = pl.ds(first, end - first)
        landed(xb.at[0, chunk, 1:4, here], x_sem[run])
        send(xb.at[0, chunk, :, here], xb.at[1, chunk, :, here], other_core, core_leaves[chunk], core_sem[run])

    def from_core(run):
        chunk, first, end = run
        landed(xb.at[1, chunk, :, pl.ds(first, end - first)], core_sem[run])

    hand_on_x(NEAR_RUNS[0])
    loads[6].wait()
    wt[0] = wgu[0].T
    hand_on_x(NEAR_RUNS[1])
    hand_on_x(NEAR_RUNS[2])
    landed(slot(-4), z_sem[-4 % 16])
    for j in (4, 3, 2, 1):
        send(slot(-4), slot(-(4 + j)), at_z(j), leaves, z_sem[-(4 + j) % 16])
    landed(slot(4), z_sem[4])
    for j in (3, 2, 1):
        send(slot(4), slot(4 + j), at_z(-j), leaves, z_sem[4 + j])
    hand_on_x(NEAR_RUNS[3])
    hand_on_x(FAR_RUNS[0])
    wt[1] = wgu[1].T
    hand_on_core(NEAR_RUNS[0])
    hand_on_core(NEAR_RUNS[1])
    hand_on_x(FAR_RUNS[1])
    hand_on_core(NEAR_RUNS[2])
    hand_on_x(FAR_RUNS[2])
    hand_on_core(NEAR_RUNS[3])
    hand_on_x(FAR_RUNS[3])
    hand_on_x(FAR_RUNS[4])

    def widen(chunk, p):
        rows = xb[p, chunk].reshape(96, GROUP, HD).reshape(96, GROUP * HD)
        xt[chunk, pl.ds(p * 96, 96), :] = rows
        wide = rows.astype(jnp.float32)
        return jnp.sum(wide * wide * inverse[...], axis=1, keepdims=True)

    lanes = lax.broadcasted_iota(jnp.int32, (96, HD), 1)
    y_sem = [(outgoing(720), take(1)) for _ in range(2)]
    h_sem = [(outgoing(288), take(1)) for _ in range(2)]

    def project(chunk, p, squares):
        high = squares.astype(jnp.bfloat16).astype(jnp.float32)
        both = jnp.where(lanes < 64, high, squares - high).astype(jnp.bfloat16)
        gu[chunk, 2 * p:2 * p + 2, :, 512:640] = both.reshape(2, 48, HD)
        rows = xt[chunk, p * 96:(p + 1) * 96]
        for k in range(2):
            part = jnp.dot(rows, wt[k], preferred_element_type=jnp.float32)
            gu[chunk, 2 * p:2 * p + 2, :, k * 256:(k + 1) * 256] = part.astype(jnp.bfloat16).reshape(2, 48, 256)
        for o in (2, 1, -1):
            target = (y + o + 4) % 4
            copy = remote(gu.at[chunk, target], yr.at[chunk, R_SLOT[-o % 4] - 1], at_y(o), *y_sem[chunk])
            pl.when(target // 2 == p)(copy.start)

    def activate(chunk):
        landed(yr.at[chunk], y_sem[chunk][1])
        v = gu[chunk, y].astype(jnp.float32)
        for i in range(3):
            v += yr[chunk, i].astype(jnp.float32)
        meansq = (v[:, 512:513] + v[:, 576:577]) * (1.0 / 8192)
        scale = lax.rsqrt(meansq + 1e-05)
        gate = v[:, :256] * scale
        up = v[:, 256:512] * scale
        hb[chunk, y] = (gate / (1.0 + jnp.exp(-gate)) * up).astype(jnp.bfloat16)
        for o in (2, 1, -1):
            send(hb.at[chunk, y], hb.at[chunk, y], at_y(o), *h_sem[chunk])

    halves = ((slice(None),), (1, 0))
    c_sem = [[(outgoing(1536 // len(h)), take(1)) for _ in h] for h in halves]
    r_sem = [[(outgoing(1152 // len(h)), take(1)) for _ in h] for h in halves]

    def down(chunk):
        landed(hb.at[chunk, 0:3], h_sem[chunk][1])
        for p in (1, 0):
            rows = hb[chunk, 2 * p:2 * p + 2].reshape(96, 256)
            wide = jnp.dot(rows, wd[...], preferred_element_type=jnp.float32).astype(jnp.bfloat16)
            po[p, chunk] = wide.reshape(96, GROUP, HD).reshape(4, 2, 192, HD)
            if p == 1:
                for half, sems in zip(halves[chunk], c_sem[chunk]):
                    send(po.at[1, chunk, :, half], dr.at[chunk, :, half], other_core, *sems)

    def reduce_core(chunk):
        for half, sems, onward in zip(halves[chunk], c_sem[chunk], r_sem[chunk]):
            landed(dr.at[chunk, :, half], sems[1])
            v = po[0, chunk, :, half].astype(jnp.float32) + dr[chunk, :, half].astype(jnp.float32)
            po[0, chunk, :, half] = v.astype(jnp.bfloat16)
            for o in (2, 1, -1):
                send(po.at[0, chunk, R_SLOT[o % 4], half], xr.at[chunk, R_SLOT[-o % 4] - 1, half], at_x(o), *onward)

    def reduce_x(chunk, i):
        half = halves[chunk][i]
        landed(xr.at[chunk, :, half], r_sem[chunk][i][1])
        v = po[0, chunk, 0, half].astype(jnp.float32)
        for k in range(3):
            v += xr[chunk, k, half].astype(jnp.float32)
        s1[chunk, half] = v.astype(jnp.bfloat16).reshape(s1.at[chunk, half].shape)

    def sums(offset):
        index = Z_SLOT[offset % 16]
        return s1.at[index // 8, index // 4 % 2, index % 4]

    last_sem = (outgoing(15 * 48), take(1))
    far_sem = [(last_sem[0], take(1)) for _ in range(2)]

    squares = widen(0, 0)
    project(0, 0, squares)
    for run in NEAR_RUNS:
        from_core(run)
    squares = widen(0, 1)
    project(0, 1, squares)
    for run in FAR_RUNS:
        hand_on_core(run)
    squares = widen(1, 0)
    project(1, 0, squares)
    activate(0)
    for run in FAR_RUNS:
        from_core(run)
    squares = widen(1, 1)
    project(1, 1, squares)
    loads[7].wait()
    down(0)
    activate(1)
    reduce_core(0)
    down(1)
    reduce_core(1)
    reduce_x(0, 0)
    for i, o in enumerate((3, -3, 2, -2, 1, -1)):
        send(sums(o), zf.at[i], at_z(o), *last_sem)
    reduce_x(1, 0)
    for o in (8, 7, -7, -6):
        j = abs(o) - 4
        send(sums(o), zi.at[j - 1 if o > 0 else 3 + j], at_z(j if o > 0 else -j), *far_sem[0 if o > 0 else 1])
    reduce_x(1, 1)
    for o in (6, 5, -5):
        j = abs(o) - 4
        send(sums(o), zi.at[j - 1 if o > 0 else 3 + j], at_z(j if o > 0 else -j), *far_sem[0 if o > 0 else 1])
    for i, (offset, first, count) in enumerate(((4, 0, 4), (-4, 4, 3))):
        landed(zi.at[pl.ds(first, count)], far_sem[i][1])
        v = sums(offset)[...].astype(jnp.float32)
        for j in range(count):
            v += zi[first + j].astype(jnp.float32)
        zacc[i] = v.astype(jnp.bfloat16)
        send(zacc.at[i], zf.at[6 + i], at_z(offset), *last_sem)
    v = sums(0)[...].astype(jnp.float32)
    landed(zf, last_sem[1])
    for i in range(8):
        v += zf[i].astype(jnp.float32)
    lay[...] = v
    for r in range(3):
        for h in range(GROUP):
            out_ref[r:r + 1, h * HD:(h + 1) * HD] = lay[pl.ds(r * GROUP + h, 1), :].astype(jnp.bfloat16)
    for leaves, rows in sent:
        landed(room.at[pl.ds(0, rows)], leaves)
    assert taken == [SENDS, LANDS], taken


def on_device(query_rows, kv_cache, lengths, residual, norm_gain, w_gate_up, w_down):
    bf16 = jnp.bfloat16
    vmem = pl.BlockSpec(memory_space=pltpu.VMEM)
    hbm = pl.BlockSpec(memory_space=pl.ANY)
    return pl.pallas_call(
        body,
        out_shape=pltpu.VMEM(query_rows.shape, bf16),
        in_specs=[hbm] * 7,
        out_specs=vmem,
        scratch_shapes=[
            pltpu.SMEM(lengths.shape, jnp.int32),
            pltpu.VMEM(query_rows.shape, bf16),
            pltpu.VMEM(residual.shape, bf16),
            pltpu.VMEM((GROUP, HD), jnp.float32),
            pltpu.VMEM(kv_cache.shape, bf16),
            pltpu.VMEM(w_gate_up.shape, bf16),
            pltpu.VMEM((2, GROUP * HD, 256), bf16),
            pltpu.VMEM(w_down.shape, bf16),
            pltpu.VMEM((48, HD), jnp.float32),
            pltpu.VMEM((1, GROUP * HD), jnp.float32),
            pltpu.VMEM((2, 2, 4, 8, 48, HD), bf16),
            pltpu.VMEM((2, 192, 2048), bf16),
            pltpu.VMEM((2, 4, 48, 640), bf16),
            pltpu.VMEM((2, 3, 48, 640), bf16),
            pltpu.VMEM((2, 4, 48, 256), bf16),
            pltpu.VMEM((2, 2, 4, 2, 192, HD), bf16),
            pltpu.VMEM((2, 4, 2, 192, HD), bf16),
            pltpu.VMEM((2, 3, 2, 192, HD), bf16),
            pltpu.VMEM((2, 2, 4, 48, HD), bf16),
            pltpu.VMEM((7, 48, HD), bf16),
            pltpu.VMEM((2, 48, HD), bf16),
            pltpu.VMEM((8, 48, HD), bf16),
            pltpu.VMEM((1536, HD), bf16),
            pltpu.SemaphoreType.DMA((8,)),
            pltpu.SemaphoreType.DMA((SENDS,)),
            pltpu.SemaphoreType.DMA((LANDS,)),
        ],
        compiler_params=pltpu.CompilerParams(
            collective_id=0, has_side_effects=True, vmem_limit_bytes=60 * 1024 * 1024
        ),
        name="decode",
    )(lengths, query_rows, residual, norm_gain.reshape(GROUP, HD), kv_cache.reshape(2, 3, -1, HD), w_gate_up, w_down)


def solution(mesh):
    return jax.shard_map(
        on_device,
        mesh=mesh,
        in_specs=(
            P(("attn", "fcol"), "frow"),
            P(None, ("attn", "fcol"), None, "frow"),
            P(("attn", "fcol")),
            P(("attn", "fcol"), "frow"),
            P("frow"),
            P(None, ("attn", "fcol"), "frow"),
            P(("attn", "fcol"), "frow"),
        ),
        out_specs=P(("attn", "fcol"), "frow"),
        check_vma=False,
    )
```

```python
import functools
import math

import jax
import jax.numpy as jnp
from jax import lax
from jax.experimental import pallas as pl
from jax.experimental.pallas import tpu as pltpu
from jax.sharding import PartitionSpec as P

HD = 128
GROUP = 16
MESH = pl.DeviceIdType.MESH
SENDS, LANDS = 5, 34
NT = (((1,), (1,)), ((), ()))

Z_OFFSETS = (0, 1, -1, 2, -2, 3, -3, 4, -4, 5, -5, 6, -6, 7, -7, 8)
Z_SLOT = {o % 16: i for i, o in enumerate(Z_OFFSETS)}
R_OFFSETS = (0, 1, -1, 2)
R_SLOT = {o % 4: i for i, o in enumerate(R_OFFSETS)}
NEAR_RUNS = ((0, 0, 1), (0, 1, 3), (0, 3, 5), (0, 5, 8))
FAR_RUNS = ((1, 0, 1), (1, 1, 3), (1, 3, 5), (1, 5, 7), (1, 7, 8))


def body(len_hbm, q_hbm, res_hbm, gain_hbm, kv_hbm, wgu_hbm, wd_hbm, out_ref,
         len_ref, q_ref, res_ref, gain_ref, kv, wgu, wt, wd, lay, inverse, xb, xt, gu, yr, hb, po, dr, xr, s1, zi, zacc, zf, room,
         local_sem, send_sem, recv_sem):
    attn = lax.axis_index("attn")
    y = lax.axis_index("frow")
    x = lax.axis_index("fcol")
    z, core = attn // 2, attn % 2

    def at_z(offset):
        return {"attn": ((z + offset + 16) % 16) * 2 + core}

    def at_x(offset):
        return {"fcol": (x + offset + 4) % 4}

    def at_y(offset):
        return {"frow": (y + offset + 4) % 4}

    other_core = {"attn": z * 2 + 1 - core}

    barrier = pltpu.get_barrier_semaphore()
    peers = [at_z(o) for o in (4, -4, 3, -3, 2, -2, 1, -1)]
    peers += [at_x(o) for o in R_OFFSETS[1:]] + [at_y(o) for o in R_OFFSETS[1:]] + [other_core]
    for peer in peers:
        pl.semaphore_signal(barrier, inc=1, device_id=peer, device_id_type=MESH)

    operands = (
        (q_hbm, q_ref), (len_hbm, len_ref), (res_hbm, res_ref), (gain_hbm, gain_ref),
        (kv_hbm.at[0], kv.at[0]), (kv_hbm.at[1], kv.at[1]), (wgu_hbm, wgu), (wd_hbm, wd),
    )
    loads = [pltpu.make_async_copy(src, dst, local_sem.at[i]) for i, (src, dst) in enumerate(operands)]
    for load in loads:
        load.start()

    taken = [0, 0]
    sent = []

    def take(kind):
        taken[kind] += 1
        return (send_sem, recv_sem)[kind].at[taken[kind] - 1]

    def outgoing(rows):
        sent.append((take(0), rows))
        return sent[-1][0]

    def remote(src, dst, peer, leaves, lands):
        return pltpu.make_async_remote_copy(
            src_ref=src, dst_ref=dst, send_sem=leaves, recv_sem=lands, device_id=peer, device_id_type=MESH
        )

    def send(src, dst, peer, leaves, lands):
        remote(src, dst, peer, leaves, lands).start()

    def landed(ref, sem):
        pltpu.make_async_copy(ref, ref, sem).wait()

    def spread(rows):
        for r in range(3):
            for h in range(GROUP):
                lay[pl.ds(r * GROUP + h, 1), :] = rows[r:r + 1, h * HD:(h + 1) * HD]
        return lay[...]

    for load in loads[:4]:
        load.wait()
    queries = spread(q_ref[...].astype(jnp.float32)).astype(jnp.bfloat16)
    residual = spread(res_ref[...].astype(jnp.float32))
    gain = gain_ref[...]
    square = 1.0 / (gain * gain)
    for h in range(GROUP):
        inverse[:, h * HD:(h + 1) * HD] = square[h:h + 1]
    loads[4].wait()
    loads[5].wait()
    rows = [slice(r * GROUP, (r + 1) * GROUP) for r in range(3)]
    positions = lax.broadcasted_iota(jnp.int32, (GROUP, kv.shape[2]), 1)
    live = jnp.concatenate([positions < len_ref[r] for r in range(3)], axis=0)
    scores = jnp.concatenate(
        [lax.dot_general(queries[rows[r]], kv[0, r], NT, preferred_element_type=jnp.float32) for r in range(3)], axis=0
    ) * (1.0 / math.sqrt(HD))
    scores = jnp.where(live, scores, -1e30)
    top = jnp.max(scores, axis=1, keepdims=True)
    expo = jnp.where(live, jnp.exp(scores - top), 0.0)
    total = jnp.sum(expo, axis=1, keepdims=True)
    probs = expo.astype(jnp.bfloat16)
    summed = jnp.concatenate(
        [jnp.dot(probs[rows[r]], kv[1, r], preferred_element_type=jnp.float32) for r in range(3)], axis=0
    )
    mixed = residual + summed / total
    xb[0, 0, 0, 0] = (mixed * jnp.concatenate([gain] * 3, axis=0)).astype(jnp.bfloat16)

    pl.semaphore_wait(barrier, len(peers))

    def slot(offset):
        index = Z_SLOT[offset % 16]
        return xb.at[0, index // 8, 0, index % 8]

    z_sem = {}
    for group in ((1, -1), (2, -2), (3, -3), (4,), (-4,), (5, -5), (6, -6), (7, -7), (8,)):
        lands = take(1)
        for o in group:
            z_sem[o % 16] = lands
    leaves = outgoing(2 * 15 * 48 + 2 * 720 + 2 * 288)
    for o in (4, -4, 3, -3, 2, -2, 1, -1):
        send(slot(0), slot(-o), at_z(o), leaves, z_sem[-o % 16])

    x_sem = {run: take(1) for run in NEAR_RUNS + FAR_RUNS}
    core_sem = [take(1), take(1)]
    x_leaves = outgoing(2 * 8 * 48 * 3)
    core_leaves = outgoing(2 * 8 * 48 * 4)

    def along_z(run, count=None):
        chunk, first, end = run
        return xb.at[0, chunk, 0, pl.ds(first, (end - first) if count is None else count)]

    def hand_on_x(run):
        chunk, first, end = run
        if run == NEAR_RUNS[3]:
            landed(along_z(run, 2), z_sem[3])
        elif run not in (NEAR_RUNS[0], FAR_RUNS[0]):
            landed(along_z(run), z_sem[Z_OFFSETS[chunk * 8 + first] % 16])
        here = pl.ds(first, end - first)
        for o in (2, 1, -1):
            send(xb.at[0, chunk, 0, here], xb.at[0, chunk, R_SLOT[-o % 4], here], at_x(o), x_leaves, x_sem[run])

    def hand_on_core(run):
        chunk, first, end = run
        here = pl.ds(first, end - first)
        landed(xb.at[0, chunk, 1:4, here], x_sem[run])
        send(xb.at[0, chunk, :, here], xb.at[1, chunk, :, here], other_core, core_leaves, core_sem[chunk])

    def from_core(chunk):
        landed(xb.at[1, chunk], core_sem[chunk])

    hand_on_x(NEAR_RUNS[0])
    loads[6].wait()
    wt[0] = wgu[0].T
    hand_on_x(NEAR_RUNS[1])
    hand_on_x(NEAR_RUNS[2])
    landed(slot(-4), z_sem[-4 % 16])
    landed(slot(4), z_sem[4])
    send(xb.at[0, 1 - core, 0, 7 * core], slot(8), at_z(4 - 8 * core), leaves, z_sem[8])
    for j in (3, 2, 1):
        send(slot(-4), slot(-(4 + j)), at_z(j), leaves, z_sem[-(4 + j) % 16])
        send(slot(4), slot(4 + j), at_z(-j), leaves, z_sem[4 + j])
    hand_on_x(NEAR_RUNS[3])
    hand_on_x(FAR_RUNS[0])
    wt[1] = wgu[1].T
    hand_on_core(NEAR_RUNS[0])
    hand_on_core(NEAR_RUNS[1])
    hand_on_x(FAR_RUNS[1])
    hand_on_core(NEAR_RUNS[2])
    hand_on_x(FAR_RUNS[2])
    hand_on_core(NEAR_RUNS[3])
    hand_on_x(FAR_RUNS[3])
    hand_on_x(FAR_RUNS[4])

    def widen(chunk, p):
        rows = xb[p, chunk].reshape(96, GROUP, HD).reshape(96, GROUP * HD)
        xt[chunk, pl.ds(p * 96, 96), :] = rows
        wide = rows.astype(jnp.float32)
        return jnp.sum(wide * wide * inverse[...], axis=1, keepdims=True)

    lanes = lax.broadcasted_iota(jnp.int32, (96, HD), 1)
    y_sem = [(leaves, take(1)) for _ in range(2)]
    h_sem = [(leaves, take(1)) for _ in range(2)]

    def block_of(row):
        return row % 2 * 2 + row // 2

    block = block_of(y)

    def project(chunk, p, squares):
        high = squares.astype(jnp.bfloat16).astype(jnp.float32)
        both = jnp.where(lanes < 64, high, squares - high).astype(jnp.bfloat16)
        gu[chunk, 2 * p:2 * p + 2, :, 512:640] = both.reshape(2, 48, HD)
        rows = xt[chunk, p * 96:(p + 1) * 96]
        for k in range(2):
            part = jnp.dot(rows, wt[k], preferred_element_type=jnp.float32)
            gu[chunk, 2 * p:2 * p + 2, :, k * 256:(k + 1) * 256] = part.astype(jnp.bfloat16).reshape(2, 48, 256)
        for o in (2, 1, -1):
            target = (y + o + 4) % 4
            copy = remote(gu.at[chunk, block_of(target)], yr.at[chunk, R_SLOT[-o % 4] - 1], at_y(o), *y_sem[chunk])
            pl.when(target % 2 == p)(copy.start)

    def activate(chunk):
        landed(yr.at[chunk], y_sem[chunk][1])
        v = gu[chunk, block].astype(jnp.float32)
        for i in range(3):
            v += yr[chunk, i].astype(jnp.float32)
        meansq = (v[:, 512:513] + v[:, 576:577]) * (1.0 / 8192)
        scale = lax.rsqrt(meansq + 1e-05)
        gate = v[:, :256] * scale
        up = v[:, 256:512] * scale
        hb[chunk, block] = (gate / (1.0 + jnp.exp(-gate)) * up).astype(jnp.bfloat16)
        for o in (2, 1, -1):
            send(hb.at[chunk, block], hb.at[chunk, block], at_y(o), *h_sem[chunk])

    halves = ((slice(None),), (1, 0))
    c_leaves, r_leaves = outgoing(2 * 1536), outgoing(2 * 1152)
    c_sem = [[(c_leaves, take(1)) for _ in h] for h in halves]
    r_sem = [[(r_leaves, take(1)) for _ in h] for h in halves]

    def down(chunk):
        landed(hb.at[chunk, 0:3], h_sem[chunk][1])
        for p in (1, 0):
            rows = hb[chunk, 2 * p:2 * p + 2].reshape(96, 256)
            wide = jnp.dot(rows, wd[...], preferred_element_type=jnp.float32).astype(jnp.bfloat16)
            po[p, chunk] = wide.reshape(96, GROUP, HD).reshape(4, 2, 192, HD)
            if p == 1:
                for half, sems in zip(halves[chunk], c_sem[chunk]):
                    send(po.at[1, chunk, :, half], dr.at[chunk, :, half], other_core, *sems)

    def reduce_core(chunk):
        for half, sems, onward in zip(halves[chunk], c_sem[chunk], r_sem[chunk]):
            landed(dr.at[chunk, :, half], sems[1])
            v = po[0, chunk, :, half].astype(jnp.float32) + dr[chunk, :, half].astype(jnp.float32)
            po[0, chunk, :, half] = v.astype(jnp.bfloat16)
            for o in (2, 1, -1):
                send(po.at[0, chunk, R_SLOT[o % 4], half], xr.at[chunk, R_SLOT[-o % 4] - 1, half], at_x(o), *onward)

    def reduce_x(chunk, i):
        half = halves[chunk][i]
        landed(xr.at[chunk, :, half], r_sem[chunk][i][1])
        v = po[0, chunk, 0, half].astype(jnp.float32)
        for k in range(3):
            v += xr[chunk, k, half].astype(jnp.float32)
        s1[chunk, half] = v.astype(jnp.bfloat16).reshape(s1.at[chunk, half].shape)

    def sums(offset):
        index = Z_SLOT[offset % 16]
        return s1.at[index // 8, index // 4 % 2, index % 4]

    last_sem = (leaves, take(1))
    far_sem = [(last_sem[0], take(1)) for _ in range(3)]

    squares = widen(0, 0)
    project(0, 0, squares)
    from_core(0)
    squares = widen(0, 1)
    project(0, 1, squares)
    for run in FAR_RUNS:
        hand_on_core(run)
    squares = widen(1, 0)
    project(1, 0, squares)
    activate(0)
    from_core(1)
    squares = widen(1, 1)
    project(1, 1, squares)
    loads[7].wait()
    down(0)
    activate(1)
    reduce_core(0)
    down(1)
    reduce_core(1)
    reduce_x(0, 0)
    for i, o in enumerate((3, -3, 2, -2, 1, -1)):
        send(sums(o), zf.at[i], at_z(o), *last_sem)
    reduce_x(1, 0)
    send(sums(8), zi.at[3], at_z(4 - 8 * core), *far_sem[2])
    for o in (7, -7, -6):
        j = abs(o) - 4
        send(sums(o), zi.at[j - 1 if o > 0 else 3 + j], at_z(j if o > 0 else -j), *far_sem[0 if o > 0 else 1])
    reduce_x(1, 1)
    for o in (6, 5, -5):
        j = abs(o) - 4
        send(sums(o), zi.at[j - 1 if o > 0 else 3 + j], at_z(j if o > 0 else -j), *far_sem[0 if o > 0 else 1])
    landed(zi.at[3], far_sem[2][1])
    farthest = zi[3].astype(jnp.float32)
    for i, (offset, first) in enumerate(((4, 0), (-4, 4))):
        landed(zi.at[pl.ds(first, 3)], far_sem[i][1])
        v = sums(offset)[...].astype(jnp.float32) + jnp.where(core == i, farthest, 0.0)
        for j in range(3):
            v += zi[first + j].astype(jnp.float32)
        zacc[i] = v.astype(jnp.bfloat16)
        send(zacc.at[i], zf.at[6 + i], at_z(offset), *last_sem)
    v = sums(0)[...].astype(jnp.float32)
    landed(zf, last_sem[1])
    for i in range(8):
        v += zf[i].astype(jnp.float32)
    lay[...] = v
    for r in range(3):
        for h in range(GROUP):
            out_ref[r:r + 1, h * HD:(h + 1) * HD] = lay[pl.ds(r * GROUP + h, 1), :].astype(jnp.bfloat16)
    for leaves, rows in sent:
        landed(room.at[pl.ds(0, rows)], leaves)
    assert taken == [SENDS, LANDS], taken


def on_device(query_rows, kv_cache, lengths, residual, norm_gain, w_gate_up, w_down):
    bf16 = jnp.bfloat16
    vmem = pl.BlockSpec(memory_space=pltpu.VMEM)
    hbm = pl.BlockSpec(memory_space=pl.ANY)
    return pl.pallas_call(
        body,
        out_shape=pltpu.VMEM(query_rows.shape, bf16),
        in_specs=[hbm] * 7,
        out_specs=vmem,
        scratch_shapes=[
            pltpu.SMEM(lengths.shape, jnp.int32),
            pltpu.VMEM(query_rows.shape, bf16),
            pltpu.VMEM(residual.shape, bf16),
            pltpu.VMEM((GROUP, HD), jnp.float32),
            pltpu.VMEM(kv_cache.shape, bf16),
            pltpu.VMEM(w_gate_up.shape, bf16),
            pltpu.VMEM((2, GROUP * HD, 256), bf16),
            pltpu.VMEM(w_down.shape, bf16),
            pltpu.VMEM((48, HD), jnp.float32),
            pltpu.VMEM((1, GROUP * HD), jnp.float32),
            pltpu.VMEM((2, 2, 4, 8, 48, HD), bf16),
            pltpu.VMEM((2, 192, 2048), bf16),
            pltpu.VMEM((2, 4, 48, 640), bf16),
            pltpu.VMEM((2, 3, 48, 640), bf16),
            pltpu.VMEM((2, 4, 48, 256), bf16),
            pltpu.VMEM((2, 2, 4, 2, 192, HD), bf16),
            pltpu.VMEM((2, 4, 2, 192, HD), bf16),
            pltpu.VMEM((2, 3, 2, 192, HD), bf16),
            pltpu.VMEM((2, 2, 4, 48, HD), bf16),
            pltpu.VMEM((7, 48, HD), bf16),
            pltpu.VMEM((2, 48, HD), bf16),
            pltpu.VMEM((8, 48, HD), bf16),
            pltpu.VMEM((3456, HD), bf16),
            pltpu.SemaphoreType.DMA((8,)),
            pltpu.SemaphoreType.DMA((SENDS,)),
            pltpu.SemaphoreType.DMA((LANDS,)),
        ],
        compiler_params=pltpu.CompilerParams(
            collective_id=0, has_side_effects=True, vmem_limit_bytes=60 * 1024 * 1024
        ),
        name="decode",
    )(lengths, query_rows, residual, norm_gain.reshape(GROUP, HD), kv_cache.reshape(2, 3, -1, HD), w_gate_up, w_down)


def solution(mesh):
    return jax.shard_map(
        on_device,
        mesh=mesh,
        in_specs=(
            P(("attn", "fcol"), "frow"),
            P(None, ("attn", "fcol"), None, "frow"),
            P(("attn", "fcol")),
            P(("attn", "fcol"), "frow"),
            P("frow"),
            P(None, ("attn", "fcol"), "frow"),
            P(("attn", "fcol"), "frow"),
        ),
        out_specs=P(("attn", "fcol"), "frow"),
        check_vma=False,
    )
```

```python
import functools
import math

import jax
import jax.numpy as jnp
from jax import lax
from jax.experimental import pallas as pl
from jax.experimental.pallas import tpu as pltpu
from jax.sharding import PartitionSpec as P

HD = 128
GROUP = 16
MESH = pl.DeviceIdType.MESH
SENDS, LANDS = 5, 36
NT = (((1,), (1,)), ((), ()))

Z_OFFSETS = (0, 1, -1, 2, -2, 3, -3, 4, -4, 5, -5, 6, -6, 7, -7, 8)
Z_SLOT = {o % 16: i for i, o in enumerate(Z_OFFSETS)}
R_OFFSETS = (0, 1, -1, 2)
R_SLOT = {o % 4: i for i, o in enumerate(R_OFFSETS)}
NEAR_RUNS = ((0, 0, 1), (0, 1, 3), (0, 3, 5), (0, 5, 8))
FAR_RUNS = ((1, 0, 1), (1, 1, 3), (1, 3, 5), (1, 5, 7), (1, 7, 8))


def body(len_hbm, q_hbm, res_hbm, gain_hbm, kv_hbm, wgu_hbm, wd_hbm, out_ref,
         len_ref, q_ref, res_ref, gain_ref, kv, wgu, wt, wd, lay, inverse, xb, xt, gu, yr, sq, sr, hb, po, dr, xr, s1, zi, zacc, zf, room,
         local_sem, send_sem, recv_sem):
    attn = lax.axis_index("attn")
    y = lax.axis_index("frow")
    x = lax.axis_index("fcol")
    z, core = attn // 2, attn % 2

    def at_z(offset):
        return {"attn": ((z + offset + 16) % 16) * 2 + core}

    def at_x(offset):
        return {"fcol": (x + offset + 4) % 4}

    def at_y(offset):
        return {"frow": (y + offset + 4) % 4}

    other_core = {"attn": z * 2 + 1 - core}

    barrier = pltpu.get_barrier_semaphore()
    peers = [at_z(o) for o in (4, -4, 3, -3, 2, -2, 1, -1)]
    peers += [at_x(o) for o in R_OFFSETS[1:]] + [at_y(o) for o in R_OFFSETS[1:]] + [other_core]
    for peer in peers:
        pl.semaphore_signal(barrier, inc=1, device_id=peer, device_id_type=MESH)

    operands = (
        (q_hbm, q_ref), (len_hbm, len_ref), (res_hbm, res_ref), (gain_hbm, gain_ref),
        (kv_hbm.at[0], kv.at[0]), (kv_hbm.at[1], kv.at[1]), (wgu_hbm, wgu), (wd_hbm, wd),
    )
    loads = [pltpu.make_async_copy(src, dst, local_sem.at[i]) for i, (src, dst) in enumerate(operands)]
    for load in loads:
        load.start()

    taken = [0, 0]
    sent = []

    def take(kind):
        taken[kind] += 1
        return (send_sem, recv_sem)[kind].at[taken[kind] - 1]

    def outgoing(rows):
        sent.append((take(0), rows))
        return sent[-1][0]

    def remote(src, dst, peer, leaves, lands):
        return pltpu.make_async_remote_copy(
            src_ref=src, dst_ref=dst, send_sem=leaves, recv_sem=lands, device_id=peer, device_id_type=MESH
        )

    def send(src, dst, peer, leaves, lands):
        remote(src, dst, peer, leaves, lands).start()

    def landed(ref, sem):
        pltpu.make_async_copy(ref, ref, sem).wait()

    def spread(rows):
        for r in range(3):
            for h in range(GROUP):
                lay[pl.ds(r * GROUP + h, 1), :] = rows[r:r + 1, h * HD:(h + 1) * HD]
        return lay[...]

    for load in loads[:4]:
        load.wait()
    queries = spread(q_ref[...].astype(jnp.float32)).astype(jnp.bfloat16)
    residual = spread(res_ref[...].astype(jnp.float32))
    gain = gain_ref[...]
    square = 1.0 / (gain * gain)
    for h in range(GROUP):
        inverse[:, h * HD:(h + 1) * HD] = square[h:h + 1]
    loads[4].wait()
    loads[5].wait()
    rows = [slice(r * GROUP, (r + 1) * GROUP) for r in range(3)]
    positions = lax.broadcasted_iota(jnp.int32, (GROUP, kv.shape[2]), 1)
    live = jnp.concatenate([positions < len_ref[r] for r in range(3)], axis=0)
    scores = jnp.concatenate(
        [lax.dot_general(queries[rows[r]], kv[0, r], NT, preferred_element_type=jnp.float32) for r in range(3)], axis=0
    ) * (1.0 / math.sqrt(HD))
    scores = jnp.where(live, scores, -1e30)
    top = jnp.max(scores, axis=1, keepdims=True)
    expo = jnp.where(live, jnp.exp(scores - top), 0.0)
    total = jnp.sum(expo, axis=1, keepdims=True)
    probs = expo.astype(jnp.bfloat16)
    summed = jnp.concatenate(
        [jnp.dot(probs[rows[r]], kv[1, r], preferred_element_type=jnp.float32) for r in range(3)], axis=0
    )
    mixed = residual + summed / total
    xb[0, 0, 0, 0] = (mixed * jnp.concatenate([gain] * 3, axis=0)).astype(jnp.bfloat16)

    pl.semaphore_wait(barrier, len(peers))

    def slot(offset):
        index = Z_SLOT[offset % 16]
        return xb.at[0, index // 8, 0, index % 8]

    z_sem = {}
    for group in ((1, -1), (2, -2), (3, -3), (4,), (-4,), (5, -5), (6, -6), (7, -7), (8,)):
        lands = take(1)
        for o in group:
            z_sem[o % 16] = lands
    leaves = outgoing(2 * 15 * 48 + 2 * 576 + 2 * 48 + 2 * 288)
    for o in (4, -4, 3, -3, 2, -2, 1, -1):
        send(slot(0), slot(-o), at_z(o), leaves, z_sem[-o % 16])

    x_sem = {run: take(1) for run in NEAR_RUNS + FAR_RUNS}
    core_sem = [take(1), take(1)]
    x_leaves = outgoing(2 * 8 * 48 * 3)
    core_leaves = outgoing(2 * 8 * 48 * 4)

    def along_z(run, count=None):
        chunk, first, end = run
        return xb.at[0, chunk, 0, pl.ds(first, (end - first) if count is None else count)]

    def hand_on_x(run):
        chunk, first, end = run
        if run == NEAR_RUNS[3]:
            landed(along_z(run, 2), z_sem[3])
        elif run not in (NEAR_RUNS[0], FAR_RUNS[0]):
            landed(along_z(run), z_sem[Z_OFFSETS[chunk * 8 + first] % 16])
        here = pl.ds(first, end - first)
        for o in (2, 1, -1):
            send(xb.at[0, chunk, 0, here], xb.at[0, chunk, R_SLOT[-o % 4], here], at_x(o), x_leaves, x_sem[run])

    def hand_on_core(run):
        chunk, first, end = run
        here = pl.ds(first, end - first)
        landed(xb.at[0, chunk, 1:4, here], x_sem[run])
        send(xb.at[0, chunk, :, here], xb.at[1, chunk, :, here], other_core, core_leaves, core_sem[chunk])

    def from_core(chunk):
        landed(xb.at[1, chunk], core_sem[chunk])

    hand_on_x(NEAR_RUNS[0])
    loads[6].wait()
    wt[0] = wgu[0].T
    hand_on_x(NEAR_RUNS[1])
    hand_on_x(NEAR_RUNS[2])
    landed(slot(-4), z_sem[-4 % 16])
    landed(slot(4), z_sem[4])
    send(xb.at[0, 1 - core, 0, 7 * core], slot(8), at_z(4 - 8 * core), leaves, z_sem[8])
    for j in (3, 2, 1):
        send(slot(-4), slot(-(4 + j)), at_z(j), leaves, z_sem[-(4 + j) % 16])
        send(slot(4), slot(4 + j), at_z(-j), leaves, z_sem[4 + j])
    hand_on_x(NEAR_RUNS[3])
    hand_on_x(FAR_RUNS[0])
    wt[1] = wgu[1].T
    hand_on_core(NEAR_RUNS[0])
    hand_on_core(NEAR_RUNS[1])
    hand_on_x(FAR_RUNS[1])
    hand_on_core(NEAR_RUNS[2])
    hand_on_x(FAR_RUNS[2])
    hand_on_core(NEAR_RUNS[3])
    hand_on_x(FAR_RUNS[3])
    hand_on_x(FAR_RUNS[4])

    def widen(chunk, p):
        rows = xb[p, chunk].reshape(96, GROUP, HD).reshape(96, GROUP * HD)
        xt[chunk, pl.ds(p * 96, 96), :] = rows
        wide = rows.astype(jnp.float32)
        return jnp.sum(wide * wide * inverse[...], axis=1, keepdims=True)

    lanes = lax.broadcasted_iota(jnp.int32, (96, HD), 1)
    diagonal = lax.broadcasted_iota(jnp.int32, (48, HD), 0) == lax.broadcasted_iota(jnp.int32, (48, HD), 1)
    upper = lax.broadcasted_iota(jnp.int32, (16, HD), 0) < 8
    y_sem = [(leaves, take(1)) for _ in range(2)]
    sq_sem = [take(1) for _ in range(2)]
    h_sem = [(leaves, take(1)) for _ in range(2)]

    def block_of(row):
        return row % 2 * 2 + row // 2

    block = block_of(y)

    def project(chunk, p, squares):
        high = squares.astype(jnp.bfloat16).astype(jnp.float32)
        both = jnp.where(lanes < 64, high, squares - high).astype(jnp.bfloat16)
        for b in range(2):
            tall = both[b * 48:(b + 1) * 48].astype(jnp.float32)
            flat = jnp.sum(jnp.where(diagonal, tall[:, 0:1], 0.0), axis=0, keepdims=True)
            rest = jnp.sum(jnp.where(diagonal, tall[:, 64:65], 0.0), axis=0, keepdims=True)
            sq[chunk, 2 * p + b] = jnp.where(upper, flat, rest).astype(jnp.bfloat16)
        rows = xt[chunk, p * 96:(p + 1) * 96]
        for k in range(2):
            part = jnp.dot(rows, wt[k], preferred_element_type=jnp.float32)
            gu[chunk, 2 * p:2 * p + 2, :, k * 256:(k + 1) * 256] = part.astype(jnp.bfloat16).reshape(2, 48, 256)
        for o in (2, 1, -1):
            target = (y + o + 4) % 4
            copy = remote(gu.at[chunk, block_of(target)], yr.at[chunk, R_SLOT[-o % 4] - 1], at_y(o), *y_sem[chunk])
            small = remote(sq.at[chunk, block_of(target)], sr.at[chunk, R_SLOT[-o % 4] - 1], at_y(o), leaves, sq_sem[chunk])
            pl.when(target % 2 == p)(small.start)
            pl.when(target % 2 == p)(copy.start)

    def activate(chunk):
        landed(yr.at[chunk], y_sem[chunk][1])
        v = gu[chunk, block].astype(jnp.float32)
        for i in range(3):
            v += yr[chunk, i].astype(jnp.float32)
        landed(sr.at[chunk], sq_sem[chunk])
        flat = sq[chunk, block].astype(jnp.float32)
        for i in range(3):
            flat += sr[chunk, i].astype(jnp.float32)
        both = flat[0:1] + flat[8:9]
        meansq = jnp.sum(jnp.where(diagonal, both, 0.0), axis=1, keepdims=True) * (1.0 / 8192)
        scale = lax.rsqrt(meansq + 1e-05)
        gate = v[:, :256] * scale
        up = v[:, 256:512] * scale
        hb[chunk, block] = (gate / (1.0 + jnp.exp(-gate)) * up).astype(jnp.bfloat16)
        for o in (2, 1, -1):
            send(hb.at[chunk, block], hb.at[chunk, block], at_y(o), *h_sem[chunk])

    halves = ((slice(None),), (1, 0))
    c_leaves, r_leaves = outgoing(2 * 1536), outgoing(2 * 1152)
    c_sem = [[(c_leaves, take(1)) for _ in h] for h in halves]
    r_sem = [[(r_leaves, take(1)) for _ in h] for h in halves]

    def down(chunk):
        landed(hb.at[chunk, 0:3], h_sem[chunk][1])
        for p in (1, 0):
            rows = hb[chunk, 2 * p:2 * p + 2].reshape(96, 256)
            wide = jnp.dot(rows, wd[...], preferred_element_type=jnp.float32).astype(jnp.bfloat16)
            po[p, chunk] = wide.reshape(96, GROUP, HD).reshape(4, 2, 192, HD)
            if p == 1:
                for half, sems in zip(halves[chunk], c_sem[chunk]):
                    send(po.at[1, chunk, :, half], dr.at[chunk, :, half], other_core, *sems)

    def reduce_core(chunk):
        for half, sems, onward in zip(halves[chunk], c_sem[chunk], r_sem[chunk]):
            landed(dr.at[chunk, :, half], sems[1])
            v = po[0, chunk, :, half].astype(jnp.float32) + dr[chunk, :, half].astype(jnp.float32)
            po[0, chunk, :, half] = v.astype(jnp.bfloat16)
            for o in (2, 1, -1):
                send(po.at[0, chunk, R_SLOT[o % 4], half], xr.at[chunk, R_SLOT[-o % 4] - 1, half], at_x(o), *onward)

    def reduce_x(chunk, i):
        half = halves[chunk][i]
        landed(xr.at[chunk, :, half], r_sem[chunk][i][1])
        v = po[0, chunk, 0, half].astype(jnp.float32)
        for k in range(3):
            v += xr[chunk, k, half].astype(jnp.float32)
        s1[chunk, half] = v.astype(jnp.bfloat16).reshape(s1.at[chunk, half].shape)

    def sums(offset):
        index = Z_SLOT[offset % 16]
        return s1.at[index // 8, index // 4 % 2, index % 4]

    last_sem = (leaves, take(1))
    far_sem = [(last_sem[0], take(1)) for _ in range(3)]

    squares = widen(0, 0)
    project(0, 0, squares)
    from_core(0)
    squares = widen(0, 1)
    project(0, 1, squares)
    for run in FAR_RUNS:
        hand_on_core(run)
    squares = widen(1, 0)
    project(1, 0, squares)
    activate(0)
    from_core(1)
    squares = widen(1, 1)
    project(1, 1, squares)
    loads[7].wait()
    down(0)
    activate(1)
    reduce_core(0)
    down(1)
    reduce_core(1)
    reduce_x(0, 0)
    for i, o in enumerate((3, -3, 2, -2, 1, -1)):
        send(sums(o), zf.at[i], at_z(o), *last_sem)
    reduce_x(1, 0)
    send(sums(8), zi.at[3], at_z(4 - 8 * core), *far_sem[2])
    for o in (7, -7, -6):
        j = abs(o) - 4
        send(sums(o), zi.at[j - 1 if o > 0 else 3 + j], at_z(j if o > 0 else -j), *far_sem[0 if o > 0 else 1])
    reduce_x(1, 1)
    for o in (6, 5, -5):
        j = abs(o) - 4
        send(sums(o), zi.at[j - 1 if o > 0 else 3 + j], at_z(j if o > 0 else -j), *far_sem[0 if o > 0 else 1])
    landed(zi.at[3], far_sem[2][1])
    farthest = zi[3].astype(jnp.float32)
    for i, (offset, first) in enumerate(((4, 0), (-4, 4))):
        landed(zi.at[pl.ds(first, 3)], far_sem[i][1])
        v = sums(offset)[...].astype(jnp.float32) + jnp.where(core == i, farthest, 0.0)
        for j in range(3):
            v += zi[first + j].astype(jnp.float32)
        zacc[i] = v.astype(jnp.bfloat16)
        send(zacc.at[i], zf.at[6 + i], at_z(offset), *last_sem)
    v = sums(0)[...].astype(jnp.float32)
    landed(zf, last_sem[1])
    for i in range(8):
        v += zf[i].astype(jnp.float32)
    lay[...] = v
    for r in range(3):
        for h in range(GROUP):
            out_ref[r:r + 1, h * HD:(h + 1) * HD] = lay[pl.ds(r * GROUP + h, 1), :].astype(jnp.bfloat16)
    for leaves, rows in sent:
        landed(room.at[pl.ds(0, rows)], leaves)
    assert taken == [SENDS, LANDS], taken


def on_device(query_rows, kv_cache, lengths, residual, norm_gain, w_gate_up, w_down):
    bf16 = jnp.bfloat16
    vmem = pl.BlockSpec(memory_space=pltpu.VMEM)
    hbm = pl.BlockSpec(memory_space=pl.ANY)
    return pl.pallas_call(
        body,
        out_shape=pltpu.VMEM(query_rows.shape, bf16),
        in_specs=[hbm] * 7,
        out_specs=vmem,
        scratch_shapes=[
            pltpu.SMEM(lengths.shape, jnp.int32),
            pltpu.VMEM(query_rows.shape, bf16),
            pltpu.VMEM(residual.shape, bf16),
            pltpu.VMEM((GROUP, HD), jnp.float32),
            pltpu.VMEM(kv_cache.shape, bf16),
            pltpu.VMEM(w_gate_up.shape, bf16),
            pltpu.VMEM((2, GROUP * HD, 256), bf16),
            pltpu.VMEM(w_down.shape, bf16),
            pltpu.VMEM((48, HD), jnp.float32),
            pltpu.VMEM((1, GROUP * HD), jnp.float32),
            pltpu.VMEM((2, 2, 4, 8, 48, HD), bf16),
            pltpu.VMEM((2, 192, 2048), bf16),
            pltpu.VMEM((2, 4, 48, 512), bf16),
            pltpu.VMEM((2, 3, 48, 512), bf16),
            pltpu.VMEM((2, 4, 16, HD), bf16),
            pltpu.VMEM((2, 3, 16, HD), bf16),
            pltpu.VMEM((2, 4, 48, 256), bf16),
            pltpu.VMEM((2, 2, 4, 2, 192, HD), bf16),
            pltpu.VMEM((2, 4, 2, 192, HD), bf16),
            pltpu.VMEM((2, 3, 2, 192, HD), bf16),
            pltpu.VMEM((2, 2, 4, 48, HD), bf16),
            pltpu.VMEM((7, 48, HD), bf16),
            pltpu.VMEM((2, 48, HD), bf16),
            pltpu.VMEM((8, 48, HD), bf16),
            pltpu.VMEM((3456, HD), bf16),
            pltpu.SemaphoreType.DMA((8,)),
            pltpu.SemaphoreType.DMA((SENDS,)),
            pltpu.SemaphoreType.DMA((LANDS,)),
        ],
        compiler_params=pltpu.CompilerParams(
            collective_id=0, has_side_effects=True, vmem_limit_bytes=60 * 1024 * 1024
        ),
        name="decode",
    )(lengths, query_rows, residual, norm_gain.reshape(GROUP, HD), kv_cache.reshape(2, 3, -1, HD), w_gate_up, w_down)


def solution(mesh):
    return jax.shard_map(
        on_device,
        mesh=mesh,
        in_specs=(
            P(("attn", "fcol"), "frow"),
            P(None, ("attn", "fcol"), None, "frow"),
            P(("attn", "fcol")),
            P(("attn", "fcol"), "frow"),
            P("frow"),
            P(None, ("attn", "fcol"), "frow"),
            P(("attn", "fcol"), "frow"),
        ),
        out_specs=P(("attn", "fcol"), "frow"),
        check_vma=False,
    )
```

```python
import functools
import math

import jax
import jax.numpy as jnp
from jax import lax
from jax.experimental import pallas as pl
from jax.experimental.pallas import tpu as pltpu
from jax.sharding import PartitionSpec as P

HD = 128
GROUP = 16
MESH = pl.DeviceIdType.MESH
SENDS, LANDS = 5, 36
NT = (((1,), (1,)), ((), ()))

Z_OFFSETS = (0, 1, -1, 2, -2, 3, -3, 4, -4, 5, -5, 6, -6, 7, -7, 8)
Z_SLOT = {o % 16: i for i, o in enumerate(Z_OFFSETS)}
R_OFFSETS = (0, 1, -1, 2)
R_SLOT = {o % 4: i for i, o in enumerate(R_OFFSETS)}
NEAR_RUNS = ((0, 0, 1), (0, 1, 3), (0, 3, 5), (0, 5, 8))
FAR_RUNS = ((1, 0, 1), (1, 1, 3), (1, 3, 5), (1, 5, 7), (1, 7, 8))


def body(len_hbm, q_hbm, res_hbm, gain_hbm, kv_hbm, wgu_hbm, wd_hbm, out_ref,
         len_ref, q_ref, res_ref, gain_ref, kv, wgu, wt, wd, lay, inverse, xb, xt, gu, yr, sq, sr, hb, po, dr, xr, s1, zi, zacc, zf, room,
         local_sem, send_sem, recv_sem):
    attn = lax.axis_index("attn")
    y = lax.axis_index("frow")
    x = lax.axis_index("fcol")
    z, core = attn // 2, attn % 2

    def at_z(offset):
        return {"attn": ((z + offset + 16) % 16) * 2 + core}

    def at_x(offset):
        return {"fcol": (x + offset + 4) % 4}

    def at_y(offset):
        return {"frow": (y + offset + 4) % 4}

    other_core = {"attn": z * 2 + 1 - core}

    barrier = pltpu.get_barrier_semaphore()
    peers = [at_z(o) for o in (4, -4, 3, -3, 2, -2, 1, -1)]
    peers += [at_x(o) for o in R_OFFSETS[1:]] + [at_y(o) for o in R_OFFSETS[1:]] + [other_core]
    for peer in peers:
        pl.semaphore_signal(barrier, inc=1, device_id=peer, device_id_type=MESH)

    operands = (
        (q_hbm, q_ref), (len_hbm, len_ref), (res_hbm, res_ref), (gain_hbm, gain_ref),
        (kv_hbm.at[0], kv.at[0]), (kv_hbm.at[1], kv.at[1]), (wgu_hbm, wgu), (wd_hbm, wd),
    )
    loads = [pltpu.make_async_copy(src, dst, local_sem.at[i]) for i, (src, dst) in enumerate(operands)]
    for load in loads:
        load.start()

    taken = [0, 0]
    sent = []

    def take(kind):
        taken[kind] += 1
        return (send_sem, recv_sem)[kind].at[taken[kind] - 1]

    def outgoing(rows):
        sent.append((take(0), rows))
        return sent[-1][0]

    def remote(src, dst, peer, leaves, lands):
        return pltpu.make_async_remote_copy(
            src_ref=src, dst_ref=dst, send_sem=leaves, recv_sem=lands, device_id=peer, device_id_type=MESH
        )

    def send(src, dst, peer, leaves, lands):
        remote(src, dst, peer, leaves, lands).start()

    def landed(ref, sem):
        pltpu.make_async_copy(ref, ref, sem).wait()

    def spread(rows):
        for r in range(3):
            for h in range(GROUP):
                lay[pl.ds(r * GROUP + h, 1), :] = rows[r:r + 1, h * HD:(h + 1) * HD]
        return lay[...]

    for load in loads[:4]:
        load.wait()
    queries = spread(q_ref[...].astype(jnp.float32)).astype(jnp.bfloat16)
    residual = spread(res_ref[...].astype(jnp.float32))
    gain = gain_ref[...]
    square = 1.0 / (gain * gain)
    for h in range(GROUP):
        inverse[:, h * HD:(h + 1) * HD] = square[h:h + 1]
    loads[4].wait()
    loads[5].wait()
    rows = [slice(r * GROUP, (r + 1) * GROUP) for r in range(3)]
    positions = lax.broadcasted_iota(jnp.int32, (GROUP, kv.shape[2]), 1)
    live = jnp.concatenate([positions < len_ref[r] for r in range(3)], axis=0)
    scores = jnp.concatenate(
        [lax.dot_general(queries[rows[r]], kv[0, r], NT, preferred_element_type=jnp.float32) for r in range(3)], axis=0
    ) * (1.0 / math.sqrt(HD))
    scores = jnp.where(live, scores, -1e30)
    top = jnp.max(scores, axis=1, keepdims=True)
    expo = jnp.where(live, jnp.exp(scores - top), 0.0)
    total = jnp.sum(expo, axis=1, keepdims=True)
    probs = expo.astype(jnp.bfloat16)
    summed = jnp.concatenate(
        [jnp.dot(probs[rows[r]], kv[1, r], preferred_element_type=jnp.float32) for r in range(3)], axis=0
    )
    mixed = residual + summed / total
    xb[0, 0, 0, 0] = (mixed * jnp.concatenate([gain] * 3, axis=0)).astype(jnp.bfloat16)

    pl.semaphore_wait(barrier, len(peers))

    def slot(offset):
        index = Z_SLOT[offset % 16]
        return xb.at[0, index // 8, 0, index % 8]

    z_sem = {}
    for group in ((1, -1), (2, -2), (3, -3), (4,), (-4,), (5, -5), (6, -6), (7, -7), (8,)):
        lands = take(1)
        for o in group:
            z_sem[o % 16] = lands
    leaves = outgoing(2 * 15 * 48 + 2 * 576 + 2 * 48 + 2 * 288)
    for o in (4, -4, 3, -3, 2, -2, 1, -1):
        send(slot(0), slot(-o), at_z(o), leaves, z_sem[-o % 16])

    x_sem = {run: take(1) for run in NEAR_RUNS + FAR_RUNS}
    core_sem = [take(1), take(1)]
    x_leaves = outgoing(2 * 8 * 48 * 3)
    core_leaves = outgoing(2 * 8 * 48 * 4)

    def along_z(run, count=None):
        chunk, first, end = run
        return xb.at[0, chunk, 0, pl.ds(first, (end - first) if count is None else count)]

    def hand_on_x(run):
        chunk, first, end = run
        if run == NEAR_RUNS[3]:
            landed(along_z(run, 2), z_sem[3])
        elif run not in (NEAR_RUNS[0], FAR_RUNS[0]):
            landed(along_z(run), z_sem[Z_OFFSETS[chunk * 8 + first] % 16])
        here = pl.ds(first, end - first)
        for o in (2, 1, -1):
            send(xb.at[0, chunk, 0, here], xb.at[0, chunk, R_SLOT[-o % 4], here], at_x(o), x_leaves, x_sem[run])

    def hand_on_core(run):
        chunk, first, end = run
        here = pl.ds(first, end - first)
        landed(xb.at[0, chunk, 1:4, here], x_sem[run])
        send(xb.at[0, chunk, :, here], xb.at[1, chunk, :, here], other_core, core_leaves, core_sem[chunk])

    def from_core(chunk):
        landed(xb.at[1, chunk], core_sem[chunk])

    hand_on_x(NEAR_RUNS[0])
    loads[6].wait()
    wt[0] = wgu[0].T
    hand_on_x(NEAR_RUNS[1])
    hand_on_x(NEAR_RUNS[2])
    landed(slot(-4), z_sem[-4 % 16])
    landed(slot(4), z_sem[4])
    send(xb.at[0, 1 - core, 0, 7 * core], slot(8), at_z(4 - 8 * core), leaves, z_sem[8])
    for j in (3, 2, 1):
        send(slot(-4), slot(-(4 + j)), at_z(j), leaves, z_sem[-(4 + j) % 16])
        send(slot(4), slot(4 + j), at_z(-j), leaves, z_sem[4 + j])
    hand_on_x(NEAR_RUNS[3])
    hand_on_x(FAR_RUNS[0])
    wt[1] = wgu[1].T
    hand_on_core(NEAR_RUNS[0])
    hand_on_core(NEAR_RUNS[1])
    hand_on_x(FAR_RUNS[1])
    hand_on_core(NEAR_RUNS[2])
    hand_on_x(FAR_RUNS[2])
    hand_on_core(NEAR_RUNS[3])
    hand_on_x(FAR_RUNS[3])
    hand_on_x(FAR_RUNS[4])

    def widen(chunk, p):
        rows = xb[p, chunk].reshape(96, GROUP, HD).reshape(96, GROUP * HD)
        xt[chunk, pl.ds(p * 96, 96), :] = rows
        wide = rows.astype(jnp.float32)
        return jnp.sum(wide * wide * inverse[...], axis=1, keepdims=True)

    lanes = lax.broadcasted_iota(jnp.int32, (96, HD), 1)
    diagonal = lax.broadcasted_iota(jnp.int32, (48, HD), 0) == lax.broadcasted_iota(jnp.int32, (48, HD), 1)
    upper = lax.broadcasted_iota(jnp.int32, (16, HD), 0) < 8
    y_sem = [(leaves, take(1)) for _ in range(2)]
    sq_sem = [take(1) for _ in range(2)]
    h_sem = [(leaves, take(1)) for _ in range(2)]

    def block_of(row):
        return row % 2 * 2 + row // 2

    block = block_of(y)

    def project(chunk, p, squares):
        high = squares.astype(jnp.bfloat16).astype(jnp.float32)
        both = jnp.where(lanes < 64, high, squares - high).astype(jnp.bfloat16)
        for b in range(2):
            tall = both[b * 48:(b + 1) * 48].astype(jnp.float32)
            flat = jnp.sum(jnp.where(diagonal, tall[:, 0:1], 0.0), axis=0, keepdims=True)
            rest = jnp.sum(jnp.where(diagonal, tall[:, 64:65], 0.0), axis=0, keepdims=True)
            sq[chunk, 2 * p + b] = jnp.where(upper, flat, rest).astype(jnp.bfloat16)
        rows = xt[chunk, p * 96:(p + 1) * 96]
        targets = [(o, (y + o + 4) % 4) for o in (2, 1, -1)]
        for o, target in targets:
            small = remote(sq.at[chunk, block_of(target)], sr.at[chunk, R_SLOT[-o % 4] - 1], at_y(o), leaves, sq_sem[chunk])
            pl.when(target % 2 == p)(small.start)
        for k in range(2):
            columns = pl.ds(k * 256, 256)
            part = jnp.dot(rows, wt[k], preferred_element_type=jnp.float32)
            gu[chunk, 2 * p:2 * p + 2, :, k * 256:(k + 1) * 256] = part.astype(jnp.bfloat16).reshape(2, 48, 256)
            for o, target in targets:
                copy = remote(
                    gu.at[chunk, block_of(target), :, columns], yr.at[chunk, R_SLOT[-o % 4] - 1, :, columns],
                    at_y(o), *y_sem[chunk],
                )
                pl.when(target % 2 == p)(copy.start)

    def activate(chunk):
        landed(yr.at[chunk], y_sem[chunk][1])
        v = gu[chunk, block].astype(jnp.float32)
        for i in range(3):
            v += yr[chunk, i].astype(jnp.float32)
        landed(sr.at[chunk], sq_sem[chunk])
        flat = sq[chunk, block].astype(jnp.float32)
        for i in range(3):
            flat += sr[chunk, i].astype(jnp.float32)
        both = flat[0:1] + flat[8:9]
        meansq = jnp.sum(jnp.where(diagonal, both, 0.0), axis=1, keepdims=True) * (1.0 / 8192)
        scale = lax.rsqrt(meansq + 1e-05)
        gate = v[:, :256] * scale
        up = v[:, 256:512] * scale
        hb[chunk, block] = (gate / (1.0 + jnp.exp(-gate)) * up).astype(jnp.bfloat16)
        for o in (2, 1, -1):
            send(hb.at[chunk, block], hb.at[chunk, block], at_y(o), *h_sem[chunk])

    halves = ((slice(None),), (1, 0))
    c_leaves, r_leaves = outgoing(2 * 1536), outgoing(2 * 1152)
    c_sem = [[(c_leaves, take(1)) for _ in h] for h in halves]
    r_sem = [[(r_leaves, take(1)) for _ in h] for h in halves]

    def down(chunk):
        landed(hb.at[chunk, 0:3], h_sem[chunk][1])
        for p in (1, 0):
            rows = hb[chunk, 2 * p:2 * p + 2].reshape(96, 256)
            wide = jnp.dot(rows, wd[...], preferred_element_type=jnp.float32).astype(jnp.bfloat16)
            po[p, chunk] = wide.reshape(96, GROUP, HD).reshape(4, 2, 192, HD)
            if p == 1:
                for half, sems in zip(halves[chunk], c_sem[chunk]):
                    send(po.at[1, chunk, :, half], dr.at[chunk, :, half], other_core, *sems)

    def reduce_core(chunk):
        for half, sems, onward in zip(halves[chunk], c_sem[chunk], r_sem[chunk]):
            landed(dr.at[chunk, :, half], sems[1])
            v = po[0, chunk, :, half].astype(jnp.float32) + dr[chunk, :, half].astype(jnp.float32)
            po[0, chunk, :, half] = v.astype(jnp.bfloat16)
            for o in (2, 1, -1):
                send(po.at[0, chunk, R_SLOT[o % 4], half], xr.at[chunk, R_SLOT[-o % 4] - 1, half], at_x(o), *onward)

    def reduce_x(chunk, i):
        half = halves[chunk][i]
        landed(xr.at[chunk, :, half], r_sem[chunk][i][1])
        v = po[0, chunk, 0, half].astype(jnp.float32)
        for k in range(3):
            v += xr[chunk, k, half].astype(jnp.float32)
        s1[chunk, half] = v.astype(jnp.bfloat16).reshape(s1.at[chunk, half].shape)

    def sums(offset):
        index = Z_SLOT[offset % 16]
        return s1.at[index // 8, index // 4 % 2, index % 4]

    last_sem = (leaves, take(1))
    far_sem = [(last_sem[0], take(1)) for _ in range(3)]

    squares = widen(0, 0)
    project(0, 0, squares)
    from_core(0)
    squares = widen(0, 1)
    project(0, 1, squares)
    for run in FAR_RUNS:
        hand_on_core(run)
    squares = widen(1, 0)
    project(1, 0, squares)
    activate(0)
    from_core(1)
    squares = widen(1, 1)
    project(1, 1, squares)
    loads[7].wait()
    down(0)
    activate(1)
    reduce_core(0)
    down(1)
    reduce_core(1)
    reduce_x(0, 0)
    for i, o in enumerate((3, -3, 2, -2, 1, -1)):
        send(sums(o), zf.at[i], at_z(o), *last_sem)
    reduce_x(1, 0)
    send(sums(8), zi.at[3], at_z(4 - 8 * core), *far_sem[2])
    for o in (7, -7, -6):
        j = abs(o) - 4
        send(sums(o), zi.at[j - 1 if o > 0 else 3 + j], at_z(j if o > 0 else -j), *far_sem[0 if o > 0 else 1])
    reduce_x(1, 1)
    for o in (6, 5, -5):
        j = abs(o) - 4
        send(sums(o), zi.at[j - 1 if o > 0 else 3 + j], at_z(j if o > 0 else -j), *far_sem[0 if o > 0 else 1])
    landed(zi.at[3], far_sem[2][1])
    farthest = zi[3].astype(jnp.float32)
    for i, (offset, first) in enumerate(((4, 0), (-4, 4))):
        landed(zi.at[pl.ds(first, 3)], far_sem[i][1])
        v = sums(offset)[...].astype(jnp.float32) + jnp.where(core == i, farthest, 0.0)
        for j in range(3):
            v += zi[first + j].astype(jnp.float32)
        zacc[i] = v.astype(jnp.bfloat16)
        send(zacc.at[i], zf.at[6 + i], at_z(offset), *last_sem)
    v = sums(0)[...].astype(jnp.float32)
    landed(zf, last_sem[1])
    for i in range(8):
        v += zf[i].astype(jnp.float32)
    lay[...] = v
    for r in range(3):
        for h in range(GROUP):
            out_ref[r:r + 1, h * HD:(h + 1) * HD] = lay[pl.ds(r * GROUP + h, 1), :].astype(jnp.bfloat16)
    for leaves, rows in sent:
        landed(room.at[pl.ds(0, rows)], leaves)
    assert taken == [SENDS, LANDS], taken


def on_device(query_rows, kv_cache, lengths, residual, norm_gain, w_gate_up, w_down):
    bf16 = jnp.bfloat16
    vmem = pl.BlockSpec(memory_space=pltpu.VMEM)
    hbm = pl.BlockSpec(memory_space=pl.ANY)
    return pl.pallas_call(
        body,
        out_shape=pltpu.VMEM(query_rows.shape, bf16),
        in_specs=[hbm] * 7,
        out_specs=vmem,
        scratch_shapes=[
            pltpu.SMEM(lengths.shape, jnp.int32),
            pltpu.VMEM(query_rows.shape, bf16),
            pltpu.VMEM(residual.shape, bf16),
            pltpu.VMEM((GROUP, HD), jnp.float32),
            pltpu.VMEM(kv_cache.shape, bf16),
            pltpu.VMEM(w_gate_up.shape, bf16),
            pltpu.VMEM((2, GROUP * HD, 256), bf16),
            pltpu.VMEM(w_down.shape, bf16),
            pltpu.VMEM((48, HD), jnp.float32),
            pltpu.VMEM((1, GROUP * HD), jnp.float32),
            pltpu.VMEM((2, 2, 4, 8, 48, HD), bf16),
            pltpu.VMEM((2, 192, 2048), bf16),
            pltpu.VMEM((2, 4, 48, 512), bf16),
            pltpu.VMEM((2, 3, 48, 512), bf16),
            pltpu.VMEM((2, 4, 16, HD), bf16),
            pltpu.VMEM((2, 3, 16, HD), bf16),
            pltpu.VMEM((2, 4, 48, 256), bf16),
            pltpu.VMEM((2, 2, 4, 2, 192, HD), bf16),
            pltpu.VMEM((2, 4, 2, 192, HD), bf16),
            pltpu.VMEM((2, 3, 2, 192, HD), bf16),
            pltpu.VMEM((2, 2, 4, 48, HD), bf16),
            pltpu.VMEM((7, 48, HD), bf16),
            pltpu.VMEM((2, 48, HD), bf16),
            pltpu.VMEM((8, 48, HD), bf16),
            pltpu.VMEM((3456, HD), bf16),
            pltpu.SemaphoreType.DMA((8,)),
            pltpu.SemaphoreType.DMA((SENDS,)),
            pltpu.SemaphoreType.DMA((LANDS,)),
        ],
        compiler_params=pltpu.CompilerParams(
            collective_id=0, has_side_effects=True, vmem_limit_bytes=60 * 1024 * 1024
        ),
        name="decode",
    )(lengths, query_rows, residual, norm_gain.reshape(GROUP, HD), kv_cache.reshape(2, 3, -1, HD), w_gate_up, w_down)


def solution(mesh):
    return jax.shard_map(
        on_device,
        mesh=mesh,
        in_specs=(
            P(("attn", "fcol"), "frow"),
            P(None, ("attn", "fcol"), None, "frow"),
            P(("attn", "fcol")),
            P(("attn", "fcol"), "frow"),
            P("frow"),
            P(None, ("attn", "fcol"), "frow"),
            P(("attn", "fcol"), "frow"),
        ),
        out_specs=P(("attn", "fcol"), "frow"),
        check_vma=False,
    )
```
